128 devices in a mesh: seq: 8 (over x, y_hi), tensor: 16 (over z, y_lo, core).
Axes of the slice: x: 4, y: 4 (y_hi: 2, y_lo: 2; y = y_hi * 2 + y_lo), z: 4, core: 2. Of those that a mesh axis runs over, the one named last changes fastest.
Arguments:
- activations: bfloat16 [8192, 2048], P('seq', 'tensor'), may hold values from -6 to 6
- bases: int32 [8192], P('seq'), may hold values from 0 to 4
- complement: int32 [5], replicated, may hold values from 0 to 4, each once
- embedding: bfloat16 [5, 2048], replicated, may hold values from -6 to 6
- filter_taps: bfloat16 [255, 2048], P(None, 'tensor'), may hold values from -0.375 to 0.375
- projection: bfloat16 [2048, 2048], P('tensor'), may hold values from -0.125 to 0.125
Outputs:
- mixed: bfloat16 [8192, 2048], P('seq', 'tensor')
The draws below stay inside these ranges and needn't reach their ends.
Inputs may be any that keep to these rules, and one draw needn't show every extreme that they name: `complement`: each of the 5 ids appears once.
All inputs are finite; a program needn't handle non-finite values.
Results may differ from the reference program's by a relative error of at most 0.0085.
Values may be sent and summed in bfloat16 or wider, within the bound.
A program may use at most 320 MiB of HBM per device.

```python
import jax
import jax.numpy as jnp

D = 2048
TAPS = 255
VOCAB = 5
LENGTH = 8192


def touch_ends(values, key, low, top_value):
    spot = [jax.random.randint(jax.random.fold_in(key, axis), (), 0, length) for axis, length in enumerate(values.shape)]
    widest = values.shape.index(max(values.shape))
    next_to = spot[:widest] + [(spot[widest] + 1) % values.shape[widest]] + spot[widest + 1:]
    return values.at[tuple(spot)].set(low).at[tuple(next_to)].set(top_value)


def shard_levels(rng, extent, shards, smallest, high):
    level = 1.0
    for position, blocks in shards:
        heights = jax.random.uniform(jax.random.fold_in(jax.random.fold_in(rng, 6), position), (blocks,), jnp.float32, smallest / len(shards), high / len(shards))
        level = level * jnp.repeat(jnp.exp(heights), extent[position] // blocks).reshape((-1,) + (1,) * (len(extent) - 1 - position))
    return level


def bell_draw(rng, shape, spread, limit, cuts=(), held_as=jnp.bfloat16):
    loudness = shard_levels(rng, shape, cuts, -0.22, 0.18) if cuts else 1.0
    drawn = jax.random.normal(rng, shape, jnp.float32) * spread * loudness
    return jnp.minimum(jnp.maximum(drawn, -limit), limit).astype(held_as)


def setup_inputs(seed: int = 0) -> dict:
    keys = jax.random.split(jax.random.key(seed), 7)
    return {
        "activations": bell_draw(keys[0], (LENGTH, D), 1.0, 6.0, ((0, 8), (1, 16))),
        "bases": touch_ends(jax.random.randint(keys[1], (LENGTH,), 0, VOCAB), jax.random.fold_in(keys[1], 1), 0, VOCAB - 1).astype(jnp.int32),
        "complement": jax.random.permutation(keys[2], VOCAB).astype(jnp.int32),
        "embedding": bell_draw(keys[3], (VOCAB, D), 1.0, 6.0),
        "filter_taps": bell_draw(keys[4], (TAPS, D), TAPS ** -0.5, 0.375, ((1, 16),)),
        "projection": bell_draw(keys[5], (D, D), D ** -0.5, 0.125, ((0, 16),)),
    }


def depthwise(field, filter_taps):
    row_count = field.shape[0]
    taps_count = filter_taps.shape[0]
    half_width = (taps_count - 1) // 2
    fft_size = 1 << (row_count + taps_count).bit_length()
    spectrum = jnp.fft.rfft(field.astype(jnp.float32), fft_size, axis=0)
    kernel = jnp.fft.rfft(filter_taps.astype(jnp.float32)[::-1], fft_size, axis=0)
    full = jnp.fft.irfft(spectrum * kernel, fft_size, axis=0)
    return full[half_width:half_width + row_count].astype(jnp.float32)


def activate(field, filter_taps):
    return jax.nn.gelu(depthwise(field, filter_taps), approximate=False).astype(jnp.bfloat16)


def reference(activations, bases, complement, embedding, filter_taps, projection):
    table = embedding.astype(jnp.float32)
    forward_rows = (activations.astype(jnp.float32) + table[bases]).astype(jnp.bfloat16)
    mirrored_ids = complement[bases[::-1]]
    backward_rows = (activations[::-1, ::-1].astype(jnp.float32) + table[mirrored_ids]).astype(jnp.bfloat16)
    forward_act = activate(forward_rows, filter_taps)
    backward_act = activate(backward_rows, filter_taps)
    forward_sum = jnp.dot(forward_act, projection, preferred_element_type=jnp.float32)
    backward_sum = jnp.dot(backward_act, projection, preferred_element_type=jnp.float32)
    return (forward_sum + backward_sum[::-1, ::-1]).astype(jnp.bfloat16)
```

```python
import functools

import jax
import jax.numpy as jnp
import numpy as np
from jax import lax
from jax.experimental import pallas as pl
from jax.experimental.pallas import tpu as pltpu
from jax.sharding import PartitionSpec as P

MESH = pl.DeviceIdType.MESH
F32, BF16 = jnp.float32, jnp.bfloat16
LANES = 128
BLOCK = 256
WINDOW = 2 * BLOCK


def split_table(table):
    high = table.astype(BF16)
    low = (table - high.astype(np.float64)).astype(BF16)
    return high, low


def dft_tables(taps_count):
    frequency = np.arange(BLOCK)[:, None]
    place = np.arange(WINDOW)[None, :]
    angle = 2 * np.pi / WINDOW * (frequency * place % WINDOW)
    sines = -np.sin(angle)
    sines[0] = 1.0 - 2.0 * (np.arange(WINDOW) % 2)
    analysis = np.concatenate([np.cos(angle), sines], axis=0)
    taps_forward = analysis[:, :BLOCK].copy()
    taps_forward[:, taps_count:] = 0
    taps_backward = np.zeros((WINDOW, BLOCK))
    taps_backward[:, :taps_count] = taps_forward[:, :taps_count][:, ::-1]
    taps_tables = np.concatenate([taps_forward, taps_backward], axis=0)[:, :taps_count]
    out_place = np.arange(BLOCK)[:, None] + (BLOCK - taps_count)
    out_angle = 2 * np.pi / WINDOW * (out_place * np.arange(BLOCK)[None, :] % WINDOW)
    cosines = 2 * np.cos(out_angle) / WINDOW
    cosines[:, 0] = 1.0 / WINDOW
    sines = -2 * np.sin(out_angle) / WINDOW
    sines[:, 0] = (1.0 - 2.0 * (out_place[:, 0] % 2)) / WINDOW
    synthesis = np.concatenate([cosines, sines], axis=1)
    return *split_table(analysis), *split_table(taps_tables), *split_table(synthesis)


def dot(a, b):
    return jnp.dot(a, b, preferred_element_type=F32)


def gelu(v):
    return v * (0.5 + 0.5 * lax.erf(v * np.float32(np.sqrt(0.5))))


def kernel(
    acts_ref, bases_ref, complement_ref, embedding_ref, taps_ref, weight_ref,
    flip_ref, fwd_hi, fwd_lo, tap_hi, tap_lo, inv_hi, inv_lo,
    out_ref,
    halo, bases_halo, mirror, mirror_halo, weight_far,
    table, coef, rows, wide, near, far,
    two_send, two_plus, two_minus, plus_send, minus_send, plus_recv, minus_recv, y_send, y_recv, y_keep,
    send_sem, recv_sem,
):
    seq, tensor = lax.axis_index("seq"), lax.axis_index("tensor")
    seq_count = lax.axis_size("seq")
    z, y, core = tensor // 4, (tensor // 2) % 2, tensor % 2
    right, left = lax.rem(seq + 1, seq_count), lax.rem(seq + seq_count - 1, seq_count)
    opposite = 15 - tensor
    z_plus, z_minus, z_two = lax.rem(z + 1, 4), lax.rem(z + 3, 4), lax.rem(z + 2, 4)
    at_plus = (seq, z_plus * 4 + y * 2 + core)
    at_minus = (seq, z_minus * 4 + y * 2 + core)
    at_core = (seq, z * 4 + y * 2 + (1 - core))
    at_y = (seq, z * 4 + (1 - y) * 2 + core)
    partners = [
        (right, tensor), (left, tensor), (seq, opposite), (right, opposite), (left, opposite),
        at_plus, at_minus, at_core, at_y,
    ]
    barrier = pltpu.get_barrier_semaphore()
    for partner in partners:
        pl.semaphore_signal(barrier, inc=1, device_id=partner, device_id_type=MESH)
    pl.semaphore_wait(barrier, len(partners))

    count = [0]

    def send(source, target, device):
        index = count[0]
        count[0] += 1
        copy = pltpu.make_async_remote_copy(
            src_ref=source, dst_ref=target, send_sem=send_sem.at[index], recv_sem=recv_sem.at[index],
            device_id=device, device_id_type=MESH,
        )
        copy.start()
        return copy

    length = acts_ref.shape[0]
    blocks = length // BLOCK
    first, last = pl.ds(0, LANES), pl.ds(length - LANES, LANES)
    starts = [send(acts_ref.at[last], mirror_halo.at[0], (right, opposite))]
    bounds = [0, 384, 640, 896, 1024]
    pieces = [
        send(acts_ref.at[pl.ds(a, b - a)], mirror.at[pl.ds(a, b - a)], (seq, opposite))
        for a, b in zip(bounds[:-1], bounds[1:])
    ]
    starts.append(send(acts_ref.at[first], mirror_halo.at[1], (left, opposite)))
    edges = [
        send(acts_ref.at[last], halo.at[0], (right, tensor)),
        send(bases_ref, bases_halo.at[0], (right, tensor)),
        send(acts_ref.at[first], halo.at[1], (left, tensor)),
        send(bases_ref, bases_halo.at[1], (left, tensor)),
    ]
    weight_copy = send(weight_ref, weight_far, at_core)

    taps = taps_ref[...]
    spectrum = dot(tap_hi[...], taps) + dot(tap_lo[...], taps)
    for strand in range(2):
        lanes = pl.ds(strand * LANES, LANES)
        real = spectrum[strand * WINDOW : strand * WINDOW + BLOCK]
        imag = spectrum[strand * WINDOW + BLOCK : (strand + 1) * WINDOW]
        top = lax.broadcasted_iota(jnp.int32, (BLOCK, LANES), 0) == 0
        coef[0, :, lanes] = real
        coef[1, :, lanes] = jnp.where(top, 0.0, imag)
        coef[2, :, lanes] = jnp.where(top, imag, real)

    own = embedding_ref[:, pl.ds(pl.multiple_of(tensor * LANES, LANES), LANES)].astype(F32)
    vocab = own.shape[0]
    table[...] = jnp.zeros_like(table)
    for base in range(vocab):
        table[base : base + 1, 0:LANES] = own[base : base + 1]
        row = jnp.zeros((1, LANES), F32)
        for other in range(vocab):
            weight = (complement_ref[base] == other).astype(F32)
            row = row + weight * own[other : other + 1]
        table[base : base + 1, LANES:] = row
    flip = flip_ref[...]

    def widen(source, half):
        for z_at in range(4):
            for y_at in range(2):
                chunk = z_at * 4 + y_at * 2 + core
                columns = pl.ds(pl.multiple_of(chunk * LANES, LANES), LANES)
                mirrored = pl.ds(pl.multiple_of((15 - chunk) * LANES, LANES), LANES)
                place = pl.ds(y_at * LANES, LANES)
                wide[z_at, pl.ds(half * BLOCK, LANES), place] = source[:, columns]
                wide[z_at, pl.ds(half * BLOCK + LANES, LANES), place] = dot(source[:, mirrored], flip).astype(BF16)

    widen(weight_ref, 0)
    bases_table = table[...].astype(BF16)

    def form_rows(group):
        if group == 0:
            plain, mirrored, ids = halo[0], mirror_halo[0], bases_halo[0, 7:8, :]
            keep = seq > 0
        elif group == 9:
            plain, mirrored, ids = halo[1], mirror_halo[1], bases_halo[1, 0:1, :]
            keep = seq < seq_count - 1
        else:
            part = pl.ds((group - 1) * LANES, LANES)
            plain, mirrored, ids = acts_ref[part], mirror[part], bases_ref[group - 1 : group, :]
            keep = None
        hot = (lax.broadcasted_iota(jnp.int32, (16, LANES), 0) == ids).astype(F32).astype(BF16)
        added = lax.dot_general(hot, bases_table, (((0,), (0,)), ((), ())), preferred_element_type=F32)
        both = jnp.concatenate([plain.astype(F32), dot(mirrored, flip)], axis=1) + added
        if keep is not None:
            both = jnp.where(keep, both, 0.0)
        rows[pl.ds(group * LANES, LANES), :] = both.astype(BF16)

    def conv(block):
        window = rows[pl.ds(block * BLOCK, WINDOW), :]
        field = dot(fwd_hi[...], window) + dot(fwd_lo[...], window)
        real, imag = field[:BLOCK], field[BLOCK:]
        cross = coef[1]
        product = jnp.concatenate([real * coef[0] + imag * cross, imag * coef[2] - real * cross], axis=0)
        high = product.astype(BF16)
        low = (product - high.astype(F32)).astype(BF16)
        filtered = dot(inv_hi[...], high) + dot(inv_lo[...], high) + dot(inv_hi[...], low)
        near[block] = gelu(filtered).astype(BF16)
        return send(near.at[block], far.at[block], at_core)

    def project(block, z_at, low, high):
        return dot(near[block, low:high, :], wide[z_at, 0:BLOCK, :]) + dot(
            far[block, low:high, :], wide[z_at, BLOCK:, :]
        )

    half = BLOCK // 2
    two, plain, added = {}, {}, {}

    def begin(block):
        two_send[block] = project(block, z_two, 0, BLOCK).astype(BF16)
        two[block] = (
            send(two_send.at[block, pl.ds(0, half)], two_plus.at[block], at_plus),
            send(two_send.at[block, pl.ds(half, half)], two_minus.at[block], at_minus),
        )
        plus_send[block, half:, :] = project(block, z_plus, half, BLOCK).astype(BF16)
        plain_plus = send(plus_send.at[block, pl.ds(half, half)], plus_recv.at[block, pl.ds(half, half)], at_plus)
        minus_send[block, :half, :] = project(block, z_minus, 0, half).astype(BF16)
        plain_minus = send(minus_send.at[block, pl.ds(0, half)], minus_recv.at[block, pl.ds(0, half)], at_minus)
        plain[block] = (plain_plus, plain_minus)

    def accumulate(block):
        two[block][0].wait_recv()
        total = project(block, z_plus, 0, half) + two_plus[block].astype(F32)
        plus_send[block, :half, :] = total.astype(BF16)
        added_plus = send(plus_send.at[block, pl.ds(0, half)], plus_recv.at[block, pl.ds(0, half)], at_plus)
        two[block][1].wait_recv()
        total = project(block, z_minus, half, BLOCK) + two_minus[block].astype(F32)
        minus_send[block, half:, :] = total.astype(BF16)
        added_minus = send(minus_send.at[block, pl.ds(half, half)], minus_recv.at[block, pl.ds(half, half)], at_minus)
        added[block] = (added_plus, added_minus)

    crossed = {}

    def finish(block):
        total = project(block, z, 0, BLOCK)
        for copy in plain[block] + added[block]:
            copy.wait_recv()
        total = total + plus_recv[block].astype(F32) + minus_recv[block].astype(F32)
        low, high = total[:, :LANES], total[:, LANES:]
        y_keep[block] = jnp.where(y == 0, low, high)
        y_send[block] = jnp.where(y == 0, high, low).astype(BF16)
        crossed[block] = send(y_send.at[block], y_recv.at[block], at_y)

    def emit(block):
        crossed[block].wait_recv()
        out_ref[pl.ds(block * BLOCK, BLOCK), :] = (y_keep[block] + y_recv[block].astype(F32)).astype(BF16)

    for copy in edges[:2]:
        copy.wait_recv()
    starts[0].wait_recv()
    pieces[0].wait_recv()
    for group in range(4):
        form_rows(group)
    cores = [conv(0)]
    pieces[1].wait_recv()
    form_rows(4)
    form_rows(5)
    cores.append(conv(1))
    weight_copy.wait_recv()
    widen(weight_far, 1)
    cores[0].wait_recv()
    begin(0)
    pieces[2].wait_recv()
    form_rows(6)
    form_rows(7)
    cores.append(conv(2))
    cores[1].wait_recv()
    begin(1)
    accumulate(0)
    for copy in edges[2:]:
        copy.wait_recv()
    pieces[3].wait_recv()
    starts[1].wait_recv()
    form_rows(8)
    form_rows(9)
    cores.append(conv(3))
    cores[2].wait_recv()
    begin(2)
    accumulate(1)
    finish(0)
    cores[3].wait_recv()
    begin(3)
    accumulate(2)
    finish(1)
    emit(0)
    accumulate(3)
    finish(2)
    emit(1)
    finish(3)
    emit(2)
    emit(3)
    for copy in starts + pieces + edges + [weight_copy] + cores:
        copy.wait_send()
    for block in range(blocks):
        for copy in two[block] + plain[block] + added[block] + (crossed[block],):
            copy.wait_send()


def body(activations, bases, complement, embedding, filter_taps, projection):
    length, channels = activations.shape
    blocks = length // BLOCK
    copies = 11 + 8 * blocks
    tables = dft_tables(filter_taps.shape[0])
    flip = np.eye(LANES)[::-1].astype(BF16)
    vmem = pl.BlockSpec(memory_space=pltpu.VMEM)
    return pl.pallas_call(
        kernel,
        out_shape=jax.ShapeDtypeStruct((length, channels), BF16),
        in_specs=[vmem, vmem, pl.BlockSpec(memory_space=pltpu.SMEM)] + [vmem] * 10,
        out_specs=vmem,
        scratch_shapes=[
            pltpu.VMEM((2, LANES, LANES), BF16),
            pltpu.VMEM((2, 8, LANES), jnp.int32),
            pltpu.VMEM((length, LANES), BF16),
            pltpu.VMEM((2, LANES, LANES), BF16),
            pltpu.VMEM(projection.shape, BF16),
            pltpu.VMEM((16, 2 * LANES), F32),
            pltpu.VMEM((3, BLOCK, 2 * LANES), F32),
            pltpu.VMEM((length + 2 * LANES, 2 * LANES), BF16),
            pltpu.VMEM((4, 4 * LANES, 2 * LANES), BF16),
            pltpu.VMEM((blocks, BLOCK, 2 * LANES), BF16),
            pltpu.VMEM((blocks, BLOCK, 2 * LANES), BF16),
            pltpu.VMEM((blocks, BLOCK, 2 * LANES), BF16),
            pltpu.VMEM((blocks, BLOCK // 2, 2 * LANES), BF16),
            pltpu.VMEM((blocks, BLOCK // 2, 2 * LANES), BF16),
            pltpu.VMEM((blocks, BLOCK, 2 * LANES), BF16),
            pltpu.VMEM((blocks, BLOCK, 2 * LANES), BF16),
            pltpu.VMEM((blocks, BLOCK, 2 * LANES), BF16),
            pltpu.VMEM((blocks, BLOCK, 2 * LANES), BF16),
            pltpu.VMEM((blocks, BLOCK, LANES), BF16),
            pltpu.VMEM((blocks, BLOCK, LANES), BF16),
            pltpu.VMEM((blocks, BLOCK, LANES), F32),
            pltpu.SemaphoreType.DMA((copies,)),
            pltpu.SemaphoreType.DMA((copies,)),
        ],
        compiler_params=pltpu.CompilerParams(
            collective_id=0, has_side_effects=True, vmem_limit_bytes=48 * 1024 * 1024
        ),
    )(
        activations, bases.reshape(length // LANES, LANES), complement, embedding, filter_taps, projection,
        jnp.asarray(flip), *[jnp.asarray(t) for t in tables],
    )


def solution(mesh):
    placed = (P("seq", "tensor"), P("seq"), P(), P(), P(None, "tensor"), P("tensor", None))
    return jax.shard_map(
        body, mesh=mesh, in_specs=placed, out_specs=P("seq", "tensor"), check_vma=False
    )
```

```python
import functools

import jax
import jax.numpy as jnp
import numpy as np
from jax import lax
from jax.experimental import pallas as pl
from jax.experimental.pallas import tpu as pltpu
from jax.sharding import PartitionSpec as P

MESH = pl.DeviceIdType.MESH
F32, BF16 = jnp.float32, jnp.bfloat16
LANES = 128
BLOCK = 256
WINDOW = 2 * BLOCK


def split_table(table):
    high = table.astype(BF16)
    low = (table - high.astype(np.float64)).astype(BF16)
    return high, low


def dft_tables(taps_count):
    frequency = np.arange(BLOCK)[:, None]
    place = np.arange(WINDOW)[None, :]
    angle = 2 * np.pi / WINDOW * (frequency * place % WINDOW)
    sines = -np.sin(angle)
    sines[0] = 1.0 - 2.0 * (np.arange(WINDOW) % 2)
    analysis = np.concatenate([np.cos(angle), sines], axis=0)
    taps_forward = analysis[:, :BLOCK].copy()
    taps_forward[:, taps_count:] = 0
    taps_backward = np.zeros((WINDOW, BLOCK))
    taps_backward[:, :taps_count] = taps_forward[:, :taps_count][:, ::-1]
    taps_tables = np.concatenate([taps_forward, taps_backward], axis=0)[:, :taps_count]
    out_place = np.arange(BLOCK)[:, None] + (BLOCK - taps_count)
    out_angle = 2 * np.pi / WINDOW * (out_place * np.arange(BLOCK)[None, :] % WINDOW)
    cosines = 2 * np.cos(out_angle) / WINDOW
    cosines[:, 0] = 1.0 / WINDOW
    sines = -2 * np.sin(out_angle) / WINDOW
    sines[:, 0] = (1.0 - 2.0 * (out_place[:, 0] % 2)) / WINDOW
    synthesis = np.concatenate([cosines, sines], axis=1)
    return *split_table(analysis), *split_table(taps_tables), *split_table(synthesis)


def dot(a, b):
    return jnp.dot(a, b, preferred_element_type=F32)


def gelu(v):
    return v * (0.5 + 0.5 * lax.erf(v * np.float32(np.sqrt(0.5))))


def kernel(
    acts_hbm, bases_hbm, complement_hbm, embedding_hbm, taps_hbm, weight_hbm,
    flip_hbm, fwd_hi_hbm, fwd_lo_hbm, tap_hi_hbm, tap_lo_hbm, inv_hi_hbm, inv_lo_hbm,
    out_ref,
    acts_ref, bases_ref, complement_ref, embedding_ref, taps_ref, weight_ref,
    flip_ref, fwd_hi, fwd_lo, tap_hi, tap_lo, inv_hi, inv_lo,
    halo, bases_halo, mirror, mirror_halo, weight_far,
    table, coef, rows, wide, cross, near, far,
    two_send, two_plus, two_minus, plus_send, minus_send, plus_recv, minus_recv, y_send, y_recv, y_keep,
    early_send, early_recv, early_sum, late_two, late_two_plus, late_two_minus,
    late_plus_send, late_minus_send, late_plus, late_minus,
    send_sem, recv_sem, local_sem,
):
    fetched = []
    for source, target in (
        (taps_hbm, taps_ref), (tap_hi_hbm, tap_hi), (tap_lo_hbm, tap_lo), (complement_hbm, complement_ref),
        (embedding_hbm, embedding_ref), (flip_hbm, flip_ref), (weight_hbm, weight_ref), (bases_hbm, bases_ref),
        (acts_hbm, acts_ref), (fwd_hi_hbm, fwd_hi), (fwd_lo_hbm, fwd_lo), (inv_hi_hbm, inv_hi), (inv_lo_hbm, inv_lo),
    ):
        copy = pltpu.make_async_copy(source, target, local_sem.at[len(fetched)])
        copy.start()
        fetched.append(copy)

    def fetch(count):
        for copy in fetched[:count]:
            copy.wait()
        del fetched[:count]

    seq, tensor = lax.axis_index("seq"), lax.axis_index("tensor")
    seq_count = lax.axis_size("seq")
    z, y, core = tensor // 4, (tensor // 2) % 2, tensor % 2
    has_right, has_left = seq < seq_count - 1, seq > 0
    right, left = jnp.minimum(seq + 1, seq_count - 1), jnp.maximum(seq - 1, 0)
    opposite = 15 - tensor
    z_plus, z_minus, z_two = lax.rem(z + 1, 4), lax.rem(z + 3, 4), lax.rem(z + 2, 4)
    at_plus = (seq, z_plus * 4 + y * 2 + core)
    at_minus = (seq, z_minus * 4 + y * 2 + core)
    at_core = (seq, z * 4 + y * 2 + (1 - core))
    at_y = (seq, z * 4 + (1 - y) * 2 + core)
    barrier = pltpu.get_barrier_semaphore()

    def greet(*partners):
        for partner in partners:
            pl.semaphore_signal(barrier, inc=1, device_id=partner, device_id_type=MESH)

    greet((seq, opposite), at_plus, at_minus, at_core, at_y)
    pl.when(has_right)(lambda: greet((right, tensor), (right, opposite)))
    pl.when(has_left)(lambda: greet((left, tensor), (left, opposite)))
    pl.semaphore_wait(barrier, 5 + 2 * has_right.astype(jnp.int32) + 2 * has_left.astype(jnp.int32))

    count = [0]

    def plan(source, target, device):
        index = count[0]
        count[0] += 1
        return pltpu.make_async_remote_copy(
            src_ref=source, dst_ref=target, send_sem=send_sem.at[index], recv_sem=recv_sem.at[index],
            device_id=device, device_id_type=MESH,
        )

    def send(source, target, device):
        copy = plan(source, target, device)
        copy.start()
        return copy

    length = acts_hbm.shape[0]
    first, last = pl.ds(0, LANES), pl.ds(length - LANES, LANES)
    to_right = [
        plan(acts_hbm.at[last], mirror_halo.at[0], (right, opposite)),
        plan(acts_hbm.at[last], halo.at[0], (right, tensor)),
        plan(bases_hbm, bases_halo.at[0], (right, tensor)),
    ]
    to_left = [
        plan(acts_hbm.at[first], mirror_halo.at[1], (left, opposite)),
        plan(acts_hbm.at[first], halo.at[1], (left, tensor)),
        plan(bases_hbm, bases_halo.at[1], (left, tensor)),
    ]

    def each(copies, what):
        for copy in copies:
            getattr(copy, what)()

    bounds = [0, 384, 640, 896, 1024]
    pl.when(has_right)(lambda: each(to_right, "start"))
    pieces = [
        send(acts_hbm.at[pl.ds(a, b - a)], mirror.at[pl.ds(a, b - a)], (seq, opposite))
        for a, b in zip(bounds[:-1], bounds[1:])
    ]
    pl.when(has_left)(lambda: each(to_left, "start"))
    weight_copy = send(weight_hbm, weight_far, at_core)

    def blank(side):
        halo[side] = jnp.zeros_like(halo[side])
        mirror_halo[side] = jnp.zeros_like(mirror_halo[side])
        bases_halo[side] = jnp.zeros_like(bases_halo[side])

    pl.when(jnp.logical_not(has_left))(lambda: blank(0))
    pl.when(jnp.logical_not(has_right))(lambda: blank(1))

    fetch(3)
    taps = taps_ref[...]
    spectrum = dot(tap_hi[...], taps) + dot(tap_lo[...], taps)
    for strand in range(2):
        lanes = pl.ds(strand * LANES, LANES)
        real = spectrum[strand * WINDOW : strand * WINDOW + BLOCK]
        imag = spectrum[strand * WINDOW + BLOCK : (strand + 1) * WINDOW]
        top = lax.broadcasted_iota(jnp.int32, (BLOCK, LANES), 0) == 0
        coef[0, :, lanes] = real
        coef[1, :, lanes] = jnp.where(top, 0.0, imag)
        coef[2, :, lanes] = jnp.where(top, imag, real)

    fetch(3)
    own = embedding_ref[:, pl.ds(pl.multiple_of(tensor * LANES, LANES), LANES)].astype(F32)
    vocab = own.shape[0]
    table[...] = jnp.zeros_like(table)
    for base in range(vocab):
        table[base : base + 1, 0:LANES] = own[base : base + 1]
        row = jnp.zeros((1, LANES), F32)
        for other in range(vocab):
            weight = (complement_ref[base] == other).astype(F32)
            row = row + weight * own[other : other + 1]
        table[base : base + 1, LANES:] = row
    bases_table = table[...].astype(BF16)
    flip = flip_ref[...]

    def widen(source, half):
        for z_at in range(4):
            for y_at in range(2):
                chunk = z_at * 4 + y_at * 2 + core
                columns = pl.ds(pl.multiple_of(chunk * LANES, LANES), LANES)
                mirrored = pl.ds(pl.multiple_of((15 - chunk) * LANES, LANES), LANES)
                straight, turned = source[:, columns], dot(source[:, mirrored], flip).astype(BF16)
                for part, offset in ((straight, 0), (turned, LANES)):
                    depth = pl.ds(half * BLOCK + offset, LANES)
                    wide[z_at, depth, pl.ds(y_at * LANES, LANES)] = part
                    cross[y_at, depth, pl.ds(z_at * LANES, LANES)] = part

    fetch(1)
    widen(weight_ref, 0)

    def form_rows(group):
        if group == 0:
            plain, mirrored, ids = halo[0], mirror_halo[0], bases_halo[0, 7:8, :]
            keep = has_left
        elif group == 9:
            plain, mirrored, ids = halo[1], mirror_halo[1], bases_halo[1, 0:1, :]
            keep = has_right
        else:
            part = pl.ds((group - 1) * LANES, LANES)
            plain, mirrored, ids = acts_ref[part], mirror[part], bases_ref[group - 1 : group, :]
            keep = None
        hot = (lax.broadcasted_iota(jnp.int32, (16, LANES), 0) == ids).astype(F32).astype(BF16)
        added = lax.dot_general(hot, bases_table, (((0,), (0,)), ((), ())), preferred_element_type=F32)
        both = jnp.concatenate([plain.astype(F32), dot(mirrored, flip)], axis=1) + added
        if keep is not None:
            both = jnp.where(keep, both, 0.0)
        rows[pl.ds(group * LANES, LANES), :] = both.astype(BF16)

    def conv(block):
        window = rows[pl.ds(block * BLOCK, WINDOW), :]
        field = dot(fwd_hi[...], window) + dot(fwd_lo[...], window)
        real, imag = field[:BLOCK], field[BLOCK:]
        shared = coef[1]
        product = jnp.concatenate([real * coef[0] + imag * shared, imag * coef[2] - real * shared], axis=0)
        high = product.astype(BF16)
        low = (product - high.astype(F32)).astype(BF16)
        filtered = dot(inv_hi[...], high) + dot(inv_lo[...], high) + dot(inv_hi[...], low)
        near[block] = gelu(filtered).astype(BF16)
        return send(near.at[block], far.at[block], at_core)

    def project(block, weights, low, high):
        return dot(near[block, low:high, :], weights[0:BLOCK, :]) + dot(far[block, low:high, :], weights[BLOCK:, :])

    half = BLOCK // 2
    top, bottom = pl.ds(0, half), pl.ds(half, half)
    two, plain, added, crossed = {}, {}, {}, {}

    def begin(block):
        two_send[block] = project(block, wide.at[z_two], 0, BLOCK).astype(BF16)
        two[block] = (
            send(two_send.at[block, top], two_plus.at[block], at_plus),
            send(two_send.at[block, bottom], two_minus.at[block], at_minus),
        )
        plus_send[block, half:, :] = project(block, wide.at[z_plus], half, BLOCK).astype(BF16)
        plain_plus = send(plus_send.at[block, bottom], plus_recv.at[block, bottom], at_plus)
        minus_send[block, :half, :] = project(block, wide.at[z_minus], 0, half).astype(BF16)
        plain_minus = send(minus_send.at[block, top], minus_recv.at[block, top], at_minus)
        plain[block] = (plain_plus, plain_minus)

    def accumulate(block):
        total = project(block, wide.at[z_plus], 0, half)
        two[block][0].wait_recv()
        plus_send[block, :half, :] = (total + two_plus[block].astype(F32)).astype(BF16)
        added_plus = send(plus_send.at[block, top], plus_recv.at[block, top], at_plus)
        total = project(block, wide.at[z_minus], half, BLOCK)
        two[block][1].wait_recv()
        minus_send[block, half:, :] = (total + two_minus[block].astype(F32)).astype(BF16)
        added_minus = send(minus_send.at[block, bottom], minus_recv.at[block, bottom], at_minus)
        added[block] = (added_plus, added_minus)

    def finish(block):
        total = project(block, wide.at[z], 0, BLOCK)
        for copy in plain[block] + added[block]:
            copy.wait_recv()
        total = total + plus_recv[block].astype(F32) + minus_recv[block].astype(F32)
        low, high = total[:, :LANES], total[:, LANES:]
        y_keep[block] = jnp.where(y == 0, low, high)
        y_send[block] = jnp.where(y == 0, high, low).astype(BF16)
        crossed[block] = send(y_send.at[block], y_recv.at[block], at_y)

    def emit(block):
        crossed[block].wait_recv()
        out_ref[pl.ds(block * BLOCK, BLOCK), :] = (y_keep[block] + y_recv[block].astype(F32)).astype(BF16)

    early, late = [], []

    def early_begin(block):
        for part, low in ((top, 0), (bottom, half)):
            early_send[part, :] = project(block, cross.at[1 - y], low, low + half).astype(BF16)
            early.append(send(early_send.at[part], early_recv.at[part], at_y))

    def early_middle(block):
        for index, (part, low) in enumerate(((top, 0), (bottom, half))):
            total = project(block, cross.at[y], low, low + half)
            early[index].wait_recv()
            total = total + early_recv[part, :].astype(F32)
            for z_at in range(4):
                early_sum[z_at, part, :] = total[:, z_at * LANES : (z_at + 1) * LANES]
            late_two[part, :] = early_sum[z_two, part, :].astype(BF16)
            if index == 0:
                late.append(send(late_two.at[top], late_two_plus, at_plus))
                late_minus_send[top, :] = early_sum[z_minus, top, :].astype(BF16)
                late.append(send(late_minus_send.at[top], late_minus.at[top], at_minus))
            else:
                late.append(send(late_two.at[bottom], late_two_minus, at_minus))
                late_plus_send[bottom, :] = early_sum[z_plus, bottom, :].astype(BF16)
                late.append(send(late_plus_send.at[bottom], late_plus.at[bottom], at_plus))

    def early_accumulate():
        late[0].wait_recv()
        late_plus_send[top, :] = (early_sum[z_plus, top, :] + late_two_plus[...].astype(F32)).astype(BF16)
        late.append(send(late_plus_send.at[top], late_plus.at[top], at_plus))
        late[2].wait_recv()
        late_minus_send[bottom, :] = (early_sum[z_minus, bottom, :] + late_two_minus[...].astype(F32)).astype(BF16)
        late.append(send(late_minus_send.at[bottom], late_minus.at[bottom], at_minus))

    def early_emit(block):
        for index in (1, 3, 4, 5):
            late[index].wait_recv()
        total = early_sum[z] + late_plus[...].astype(F32) + late_minus[...].astype(F32)
        out_ref[pl.ds(block * BLOCK, BLOCK), :] = total.astype(BF16)

    fetch(6)
    cores = {}
    pl.when(has_left)(lambda: each(to_right, "wait_recv"))
    pieces[0].wait_recv()
    form_rows(0)
    form_rows(1)
    form_rows(2)
    form_rows(3)
    cores[0] = conv(0)
    pieces[1].wait_recv()
    form_rows(4)
    form_rows(5)
    cores[1] = conv(1)
    weight_copy.wait_recv()
    widen(weight_far, 1)
    cores[0].wait_recv()
    begin(0)
    cores[1].wait_recv()
    early_begin(1)
    pieces[2].wait_recv()
    form_rows(6)
    form_rows(7)
    cores[2] = conv(2)
    cores[2].wait_recv()
    begin(2)
    pl.when(has_right)(lambda: each(to_left, "wait_recv"))
    pieces[3].wait_recv()
    form_rows(8)
    form_rows(9)
    cores[3] = conv(3)
    cores[3].wait_recv()
    begin(3)
    accumulate(0)
    accumulate(2)
    accumulate(3)
    early_middle(1)
    finish(0)
    finish(2)
    early_accumulate()
    finish(3)
    emit(0)
    emit(2)
    early_emit(1)
    emit(3)
    pl.when(has_right)(lambda: each(to_right, "wait_send"))
    pl.when(has_left)(lambda: each(to_left, "wait_send"))
    each(pieces + [weight_copy] + list(cores.values()) + early + late, "wait_send")
    for block in (0, 2, 3):
        each(two[block] + plain[block] + added[block] + (crossed[block],), "wait_send")


def body(activations, bases, complement, embedding, filter_taps, projection):
    length, channels = activations.shape
    blocks = length // BLOCK
    copies = 48
    tables = dft_tables(filter_taps.shape[0])
    flip = np.eye(LANES)[::-1].astype(BF16)
    operands = [
        activations, bases.reshape(length // LANES, LANES), complement, embedding, filter_taps, projection,
        jnp.asarray(flip), *[jnp.asarray(t) for t in tables],
    ]
    vmem = pl.BlockSpec(memory_space=pltpu.VMEM)
    return pl.pallas_call(
        kernel,
        out_shape=jax.ShapeDtypeStruct((length, channels), BF16),
        in_specs=[pl.BlockSpec(memory_space=pl.ANY)] * len(operands),
        out_specs=vmem,
        scratch_shapes=[
            (pltpu.SMEM if operand.ndim == 1 else pltpu.VMEM)(operand.shape, operand.dtype) for operand in operands
        ]
        + [
            pltpu.VMEM((2, LANES, LANES), BF16),
            pltpu.VMEM((2, 8, LANES), jnp.int32),
            pltpu.VMEM((length, LANES), BF16),
            pltpu.VMEM((2, LANES, LANES), BF16),
            pltpu.VMEM(projection.shape, BF16),
            pltpu.VMEM((16, 2 * LANES), F32),
            pltpu.VMEM((3, BLOCK, 2 * LANES), F32),
            pltpu.VMEM((length + 2 * LANES, 2 * LANES), BF16),
            pltpu.VMEM((4, 4 * LANES, 2 * LANES), BF16),
            pltpu.VMEM((2, 4 * LANES, 4 * LANES), BF16),
            pltpu.VMEM((blocks, BLOCK, 2 * LANES), BF16),
            pltpu.VMEM((blocks, BLOCK, 2 * LANES), BF16),
            pltpu.VMEM((blocks, BLOCK, 2 * LANES), BF16),
            pltpu.VMEM((blocks, BLOCK // 2, 2 * LANES), BF16),
            pltpu.VMEM((blocks, BLOCK // 2, 2 * LANES), BF16),
            pltpu.VMEM((blocks, BLOCK, 2 * LANES), BF16),
            pltpu.VMEM((blocks, BLOCK, 2 * LANES), BF16),
            pltpu.VMEM((blocks, BLOCK, 2 * LANES), BF16),
            pltpu.VMEM((blocks, BLOCK, 2 * LANES), BF16),
            pltpu.VMEM((blocks, BLOCK, LANES), BF16),
            pltpu.VMEM((blocks, BLOCK, LANES), BF16),
            pltpu.VMEM((blocks, BLOCK, LANES), F32),
            pltpu.VMEM((BLOCK, 4 * LANES), BF16),
            pltpu.VMEM((BLOCK, 4 * LANES), BF16),
            pltpu.VMEM((4, BLOCK, LANES), F32),
            pltpu.VMEM((BLOCK, LANES), BF16),
            pltpu.VMEM((BLOCK // 2, LANES), BF16),
            pltpu.VMEM((BLOCK // 2, LANES), BF16),
            pltpu.VMEM((BLOCK, LANES), BF16),
            pltpu.VMEM((BLOCK, LANES), BF16),
            pltpu.VMEM((BLOCK, LANES), BF16),
            pltpu.VMEM((BLOCK, LANES), BF16),
            pltpu.SemaphoreType.DMA((copies,)),
            pltpu.SemaphoreType.DMA((copies,)),
            pltpu.SemaphoreType.DMA((len(operands),)),
        ],
        compiler_params=pltpu.CompilerParams(
            collective_id=0, has_side_effects=True, vmem_limit_bytes=56 * 1024 * 1024
        ),
    )(*operands)


def solution(mesh):
    placed = (P("seq", "tensor"), P("seq"), P(), P(), P(None, "tensor"), P("tensor", None))
    return jax.shard_map(
        body, mesh=mesh, in_specs=placed, out_specs=P("seq", "tensor"), check_vma=False
    )
```

```python
import functools

import jax
import jax.numpy as jnp
import numpy as np
from jax import lax
from jax.experimental import pallas as pl
from jax.experimental.pallas import tpu as pltpu
from jax.sharding import PartitionSpec as P

MESH = pl.DeviceIdType.MESH
F32, BF16 = jnp.float32, jnp.bfloat16
LANES = 128
BLOCK = 256
WINDOW = 2 * BLOCK


def split_table(table):
    high = table.astype(BF16)
    low = (table - high.astype(np.float64)).astype(BF16)
    return high, low


def dft_tables(taps_count):
    frequency = np.arange(BLOCK)[:, None]
    place = np.arange(WINDOW)[None, :]
    angle = 2 * np.pi / WINDOW * (frequency * place % WINDOW)
    sines = -np.sin(angle)
    sines[0] = 1.0 - 2.0 * (np.arange(WINDOW) % 2)
    analysis = np.concatenate([np.cos(angle), sines], axis=0)
    taps_forward = analysis[:, :BLOCK].copy()
    taps_forward[:, taps_count:] = 0
    taps_backward = np.zeros((WINDOW, BLOCK))
    taps_backward[:, :taps_count] = taps_forward[:, :taps_count][:, ::-1]
    taps_tables = np.concatenate([taps_forward, taps_backward], axis=0)[:, :taps_count]
    out_place = np.arange(BLOCK)[:, None] + (BLOCK - taps_count)
    out_angle = 2 * np.pi / WINDOW * (out_place * np.arange(BLOCK)[None, :] % WINDOW)
    cosines = 2 * np.cos(out_angle) / WINDOW
    cosines[:, 0] = 1.0 / WINDOW
    sines = -2 * np.sin(out_angle) / WINDOW
    sines[:, 0] = (1.0 - 2.0 * (out_place[:, 0] % 2)) / WINDOW
    synthesis = np.concatenate([cosines, sines], axis=1)
    return *split_table(analysis), *split_table(taps_tables), *split_table(synthesis)


def dot(a, b):
    return jnp.dot(a, b, preferred_element_type=F32)


def gelu(v):
    return v * (0.5 + 0.5 * lax.erf(v * np.float32(np.sqrt(0.5))))


def kernel(
    acts_hbm, bases_hbm, complement_hbm, embedding_hbm, taps_hbm, weight_hbm,
    flip_hbm, fwd_hi_hbm, fwd_lo_hbm, tap_hi_hbm, tap_lo_hbm, inv_hi_hbm, inv_lo_hbm,
    out_ref,
    acts_ref, bases_ref, complement_ref, embedding_ref, taps_ref, weight_ref,
    flip_ref, fwd_hi, fwd_lo, tap_hi, tap_lo, inv_hi, inv_lo,
    halo, bases_halo, mirror, mirror_halo, weight_far,
    table, coef, rows, wide, cross, near, far,
    two_send, two_plus, two_minus, plus_send, minus_send, plus_recv, minus_recv, y_send, y_recv, y_keep,
    early_send, early_recv, early_sum, late_two, late_two_plus, late_two_minus,
    late_plus_send, late_minus_send, late_plus, late_minus,
    send_sem, recv_sem, local_sem,
):
    seq, tensor = lax.axis_index("seq"), lax.axis_index("tensor")
    seq_count = lax.axis_size("seq")
    z, y, core = tensor // 4, (tensor // 2) % 2, tensor % 2
    has_right, has_left = seq < seq_count - 1, seq > 0
    right, left = jnp.minimum(seq + 1, seq_count - 1), jnp.maximum(seq - 1, 0)
    opposite = 15 - tensor
    z_plus, z_minus, z_two = lax.rem(z + 1, 4), lax.rem(z + 3, 4), lax.rem(z + 2, 4)
    at_plus = (seq, z_plus * 4 + y * 2 + core)
    at_minus = (seq, z_minus * 4 + y * 2 + core)
    at_core = (seq, z * 4 + y * 2 + (1 - core))
    at_y = (seq, z * 4 + (1 - y) * 2 + core)
    barrier = pltpu.get_barrier_semaphore()

    def greet(*partners):
        for partner in partners:
            pl.semaphore_signal(barrier, inc=1, device_id=partner, device_id_type=MESH)

    greet((seq, opposite), at_plus, at_minus, at_core, at_y)
    pl.when(has_right)(lambda: greet((right, tensor), (right, opposite)))
    pl.when(has_left)(lambda: greet((left, tensor), (left, opposite)))
    fetched = []
    for source, target in (
        (taps_hbm, taps_ref), (tap_hi_hbm, tap_hi), (tap_lo_hbm, tap_lo), (complement_hbm, complement_ref),
        (embedding_hbm, embedding_ref), (flip_hbm, flip_ref), (weight_hbm, weight_ref), (bases_hbm, bases_ref),
        (acts_hbm, acts_ref), (fwd_hi_hbm, fwd_hi), (fwd_lo_hbm, fwd_lo), (inv_hi_hbm, inv_hi), (inv_lo_hbm, inv_lo),
    ):
        copy = pltpu.make_async_copy(source, target, local_sem.at[len(fetched)])
        copy.start()
        fetched.append(copy)

    def fetch(count):
        for copy in fetched[:count]:
            copy.wait()
        del fetched[:count]

    pl.semaphore_wait(barrier, 5 + 2 * has_right.astype(jnp.int32) + 2 * has_left.astype(jnp.int32))

    count = [0]

    def plan(source, target, device):
        index = count[0]
        count[0] += 1
        return pltpu.make_async_remote_copy(
            src_ref=source, dst_ref=target, send_sem=send_sem.at[index], recv_sem=recv_sem.at[index],
            device_id=device, device_id_type=MESH,
        )

    def send(source, target, device):
        copy = plan(source, target, device)
        copy.start()
        return copy

    length = acts_hbm.shape[0]
    first, last = pl.ds(0, LANES), pl.ds(length - LANES, LANES)
    to_right = [
        plan(acts_hbm.at[last], mirror_halo.at[0], (right, opposite)),
        plan(acts_hbm.at[last], halo.at[0], (right, tensor)),
        plan(bases_hbm, bases_halo.at[0], (right, tensor)),
    ]
    to_left = [
        plan(acts_hbm.at[first], mirror_halo.at[1], (left, opposite)),
        plan(acts_hbm.at[first], halo.at[1], (left, tensor)),
        plan(bases_hbm, bases_halo.at[1], (left, tensor)),
    ]

    def each(copies, what):
        for copy in copies:
            getattr(copy, what)()

    bounds = [0, 384, 640, 896, 1024]
    pl.when(has_right)(lambda: each(to_right, "start"))
    pieces = [
        send(acts_hbm.at[pl.ds(a, b - a)], mirror.at[pl.ds(a, b - a)], (seq, opposite))
        for a, b in zip(bounds[:-1], bounds[1:])
    ]
    pl.when(has_left)(lambda: each(to_left, "start"))
    weight_copy = send(weight_hbm, weight_far, at_core)

    def blank(side):
        halo[side] = jnp.zeros_like(halo[side])
        mirror_halo[side] = jnp.zeros_like(mirror_halo[side])
        bases_halo[side] = jnp.zeros_like(bases_halo[side])

    pl.when(jnp.logical_not(has_left))(lambda: blank(0))
    pl.when(jnp.logical_not(has_right))(lambda: blank(1))

    fetch(3)
    taps = taps_ref[...]
    spectrum = dot(tap_hi[...], taps) + dot(tap_lo[...], taps)
    for strand in range(2):
        lanes = pl.ds(strand * LANES, LANES)
        real = spectrum[strand * WINDOW : strand * WINDOW + BLOCK]
        imag = spectrum[strand * WINDOW + BLOCK : (strand + 1) * WINDOW]
        top = lax.broadcasted_iota(jnp.int32, (BLOCK, LANES), 0) == 0
        coef[0, :, lanes] = real
        coef[1, :, lanes] = jnp.where(top, 0.0, imag)
        coef[2, :, lanes] = jnp.where(top, imag, real)

    fetch(3)
    own = embedding_ref[:, pl.ds(pl.multiple_of(tensor * LANES, LANES), LANES)].astype(F32)
    vocab = own.shape[0]
    table[...] = jnp.zeros_like(table)
    for base in range(vocab):
        table[base : base + 1, 0:LANES] = own[base : base + 1]
        row = jnp.zeros((1, LANES), F32)
        for other in range(vocab):
            weight = (complement_ref[base] == other).astype(F32)
            row = row + weight * own[other : other + 1]
        table[base : base + 1, LANES:] = row
    bases_table = table[...].astype(BF16)
    flip = flip_ref[...]

    def widen(source, half):
        for z_at in range(4):
            for y_at in range(2):
                chunk = z_at * 4 + y_at * 2 + core
                columns = pl.ds(pl.multiple_of(chunk * LANES, LANES), LANES)
                mirrored = pl.ds(pl.multiple_of((15 - chunk) * LANES, LANES), LANES)
                straight, turned = source[:, columns], dot(source[:, mirrored], flip).astype(BF16)
                for part, offset in ((straight, 0), (turned, LANES)):
                    depth = pl.ds(half * BLOCK + offset, LANES)
                    wide[z_at, depth, pl.ds(y_at * LANES, LANES)] = part
                    cross[y_at, depth, pl.ds(z_at * LANES, LANES)] = part

    fetch(1)
    widen(weight_ref, 0)

    def form_rows(group):
        if group == 0:
            plain, mirrored, ids = halo[0], mirror_halo[0], bases_halo[0, 7:8, :]
            keep = has_left
        elif group == 9:
            plain, mirrored, ids = halo[1], mirror_halo[1], bases_halo[1, 0:1, :]
            keep = has_right
        else:
            part = pl.ds((group - 1) * LANES, LANES)
            plain, mirrored, ids = acts_ref[part], mirror[part], bases_ref[group - 1 : group, :]
            keep = None
        hot = (lax.broadcasted_iota(jnp.int32, (16, LANES), 0) == ids).astype(F32).astype(BF16)
        added = lax.dot_general(hot, bases_table, (((0,), (0,)), ((), ())), preferred_element_type=F32)
        both = jnp.concatenate([plain.astype(F32), dot(mirrored, flip)], axis=1) + added
        if keep is not None:
            both = jnp.where(keep, both, 0.0)
        rows[pl.ds(group * LANES, LANES), :] = both.astype(BF16)

    def conv(block):
        window = rows[pl.ds(block * BLOCK, WINDOW), :]
        field = dot(fwd_hi[...], window) + dot(fwd_lo[...], window)
        real, imag = field[:BLOCK], field[BLOCK:]
        shared = coef[1]
        product = jnp.concatenate([real * coef[0] + imag * shared, imag * coef[2] - real * shared], axis=0)
        high = product.astype(BF16)
        low = (product - high.astype(F32)).astype(BF16)
        filtered = dot(inv_hi[...], high) + dot(inv_lo[...], high) + dot(inv_hi[...], low)
        near[block] = gelu(filtered).astype(BF16)
        return send(near.at[block], far.at[block], at_core)

    def project(block, weights, low, high):
        return dot(near[block, low:high, :], weights[0:BLOCK, :]) + dot(far[block, low:high, :], weights[BLOCK:, :])

    half = BLOCK // 2
    top, bottom = pl.ds(0, half), pl.ds(half, half)
    two, plain, added, crossed = {}, {}, {}, {}

    def begin(block):
        two_send[block] = project(block, wide.at[z_two], 0, BLOCK).astype(BF16)
        two[block] = (
            send(two_send.at[block, top], two_plus.at[block], at_plus),
            send(two_send.at[block, bottom], two_minus.at[block], at_minus),
        )
        plus_send[block, half:, :] = project(block, wide.at[z_plus], half, BLOCK).astype(BF16)
        plain_plus = send(plus_send.at[block, bottom], plus_recv.at[block, bottom], at_plus)
        minus_send[block, :half, :] = project(block, wide.at[z_minus], 0, half).astype(BF16)
        plain_minus = send(minus_send.at[block, top], minus_recv.at[block, top], at_minus)
        plain[block] = (plain_plus, plain_minus)

    def accumulate(block):
        total = project(block, wide.at[z_plus], 0, half)
        two[block][0].wait_recv()
        plus_send[block, :half, :] = (total + two_plus[block].astype(F32)).astype(BF16)
        added_plus = send(plus_send.at[block, top], plus_recv.at[block, top], at_plus)
        total = project(block, wide.at[z_minus], half, BLOCK)
        two[block][1].wait_recv()
        minus_send[block, half:, :] = (total + two_minus[block].astype(F32)).astype(BF16)
        added_minus = send(minus_send.at[block, bottom], minus_recv.at[block, bottom], at_minus)
        added[block] = (added_plus, added_minus)

    def finish(block):
        total = project(block, wide.at[z], 0, BLOCK)
        for copy in plain[block] + added[block]:
            copy.wait_recv()
        total = total + plus_recv[block].astype(F32) + minus_recv[block].astype(F32)
        low, high = total[:, :LANES], total[:, LANES:]
        y_keep[block] = jnp.where(y == 0, low, high)
        y_send[block] = jnp.where(y == 0, high, low).astype(BF16)
        crossed[block] = send(y_send.at[block], y_recv.at[block], at_y)

    def emit(block):
        crossed[block].wait_recv()
        out_ref[pl.ds(block * BLOCK, BLOCK), :] = (y_keep[block] + y_recv[block].astype(F32)).astype(BF16)

    early, late = [], []

    def early_begin(block):
        for part, low in ((top, 0), (bottom, half)):
            early_send[part, :] = project(block, cross.at[1 - y], low, low + half).astype(BF16)
            early.append(send(early_send.at[part], early_recv.at[part], at_y))

    def early_middle(block):
        for index, (part, low) in enumerate(((top, 0), (bottom, half))):
            total = project(block, cross.at[y], low, low + half)
            early[index].wait_recv()
            total = total + early_recv[part, :].astype(F32)
            for z_at in range(4):
                early_sum[z_at, part, :] = total[:, z_at * LANES : (z_at + 1) * LANES]
            late_two[part, :] = early_sum[z_two, part, :].astype(BF16)
            if index == 0:
                late.append(send(late_two.at[top], late_two_plus, at_plus))
                late_minus_send[top, :] = early_sum[z_minus, top, :].astype(BF16)
                late.append(send(late_minus_send.at[top], late_minus.at[top], at_minus))
            else:
                late.append(send(late_two.at[bottom], late_two_minus, at_minus))
                late_plus_send[bottom, :] = early_sum[z_plus, bottom, :].astype(BF16)
                late.append(send(late_plus_send.at[bottom], late_plus.at[bottom], at_plus))

    def early_accumulate():
        late[0].wait_recv()
        late_plus_send[top, :] = (early_sum[z_plus, top, :] + late_two_plus[...].astype(F32)).astype(BF16)
        late.append(send(late_plus_send.at[top], late_plus.at[top], at_plus))
        late[2].wait_recv()
        late_minus_send[bottom, :] = (early_sum[z_minus, bottom, :] + late_two_minus[...].astype(F32)).astype(BF16)
        late.append(send(late_minus_send.at[bottom], late_minus.at[bottom], at_minus))

    def early_emit(block):
        for index in (1, 3, 4, 5):
            late[index].wait_recv()
        total = early_sum[z] + late_plus[...].astype(F32) + late_minus[...].astype(F32)
        out_ref[pl.ds(block * BLOCK, BLOCK), :] = total.astype(BF16)

    fetch(6)
    cores = {}
    pl.when(has_left)(lambda: each(to_right, "wait_recv"))
    pieces[0].wait_recv()
    form_rows(0)
    form_rows(1)
    form_rows(2)
    form_rows(3)
    cores[0] = conv(0)
    pieces[1].wait_recv()
    form_rows(4)
    form_rows(5)
    cores[1] = conv(1)
    weight_copy.wait_recv()
    widen(weight_far, 1)
    cores[0].wait_recv()
    begin(0)
    cores[1].wait_recv()
    begin(1)
    pieces[2].wait_recv()
    form_rows(6)
    form_rows(7)
    cores[2] = conv(2)
    cores[2].wait_recv()
    early_begin(2)
    pl.when(has_right)(lambda: each(to_left, "wait_recv"))
    pieces[3].wait_recv()
    form_rows(8)
    form_rows(9)
    cores[3] = conv(3)
    accumulate(0)
    cores[3].wait_recv()
    begin(3)
    accumulate(1)
    accumulate(3)
    early_middle(2)
    finish(0)
    finish(1)
    early_accumulate()
    finish(3)
    emit(0)
    emit(1)
    early_emit(2)
    emit(3)
    pl.when(has_right)(lambda: each(to_right, "wait_send"))
    pl.when(has_left)(lambda: each(to_left, "wait_send"))
    each(pieces + [weight_copy] + list(cores.values()) + early + late, "wait_send")
    for block in sorted(two):
        each(two[block] + plain[block] + added[block] + (crossed[block],), "wait_send")


def body(activations, bases, complement, embedding, filter_taps, projection):
    length, channels = activations.shape
    blocks = length // BLOCK
    copies = 48
    tables = dft_tables(filter_taps.shape[0])
    flip = np.eye(LANES)[::-1].astype(BF16)
    operands = [
        activations, bases.reshape(length // LANES, LANES), complement, embedding, filter_taps, projection,
        jnp.asarray(flip), *[jnp.asarray(t) for t in tables],
    ]
    vmem = pl.BlockSpec(memory_space=pltpu.VMEM)
    return pl.pallas_call(
        kernel,
        out_shape=pltpu.VMEM((length, channels), BF16),
        in_specs=[pl.BlockSpec(memory_space=pl.ANY)] * len(operands),
        out_specs=vmem,
        scratch_shapes=[
            (pltpu.SMEM if operand.ndim == 1 else pltpu.VMEM)(operand.shape, operand.dtype) for operand in operands
        ]
        + [
            pltpu.VMEM((2, LANES, LANES), BF16),
            pltpu.VMEM((2, 8, LANES), jnp.int32),
            pltpu.VMEM((length, LANES), BF16),
            pltpu.VMEM((2, LANES, LANES), BF16),
            pltpu.VMEM(projection.shape, BF16),
            pltpu.VMEM((16, 2 * LANES), F32),
            pltpu.VMEM((3, BLOCK, 2 * LANES), F32),
            pltpu.VMEM((length + 2 * LANES, 2 * LANES), BF16),
            pltpu.VMEM((4, 4 * LANES, 2 * LANES), BF16),
            pltpu.VMEM((2, 4 * LANES, 4 * LANES), BF16),
            pltpu.VMEM((blocks, BLOCK, 2 * LANES), BF16),
            pltpu.VMEM((blocks, BLOCK, 2 * LANES), BF16),
            pltpu.VMEM((blocks, BLOCK, 2 * LANES), BF16),
            pltpu.VMEM((blocks, BLOCK // 2, 2 * LANES), BF16),
            pltpu.VMEM((blocks, BLOCK // 2, 2 * LANES), BF16),
            pltpu.VMEM((blocks, BLOCK, 2 * LANES), BF16),
            pltpu.VMEM((blocks, BLOCK, 2 * LANES), BF16),
            pltpu.VMEM((blocks, BLOCK, 2 * LANES), BF16),
            pltpu.VMEM((blocks, BLOCK, 2 * LANES), BF16),
            pltpu.VMEM((blocks, BLOCK, LANES), BF16),
            pltpu.VMEM((blocks, BLOCK, LANES), BF16),
            pltpu.VMEM((blocks, BLOCK, LANES), F32),
            pltpu.VMEM((BLOCK, 4 * LANES), BF16),
            pltpu.VMEM((BLOCK, 4 * LANES), BF16),
            pltpu.VMEM((4, BLOCK, LANES), F32),
            pltpu.VMEM((BLOCK, LANES), BF16),
            pltpu.VMEM((BLOCK // 2, LANES), BF16),
            pltpu.VMEM((BLOCK // 2, LANES), BF16),
            pltpu.VMEM((BLOCK, LANES), BF16),
            pltpu.VMEM((BLOCK, LANES), BF16),
            pltpu.VMEM((BLOCK, LANES), BF16),
            pltpu.VMEM((BLOCK, LANES), BF16),
            pltpu.SemaphoreType.DMA((copies,)),
            pltpu.SemaphoreType.DMA((copies,)),
            pltpu.SemaphoreType.DMA((len(operands),)),
        ],
        compiler_params=pltpu.CompilerParams(
            collective_id=0, has_side_effects=True, vmem_limit_bytes=56 * 1024 * 1024
        ),
    )(*operands)


def solution(mesh):
    placed = (P("seq", "tensor"), P("seq"), P(), P(), P(None, "tensor"), P("tensor", None))
    return jax.shard_map(
        body, mesh=mesh, in_specs=placed, out_specs=P("seq", "tensor"), check_vma=False
    )
```

```python
import functools

import jax
import jax.numpy as jnp
import numpy as np
from jax import lax
from jax.experimental import pallas as pl
from jax.experimental.pallas import tpu as pltpu
from jax.sharding import PartitionSpec as P

MESH = pl.DeviceIdType.MESH
F32, BF16 = jnp.float32, jnp.bfloat16
LANES = 128
BLOCK = 256
WINDOW = 2 * BLOCK


def split_table(table):
    high = table.astype(BF16)
    low = (table - high.astype(np.float64)).astype(BF16)
    return high, low


def dft_tables(taps_count):
    frequency = np.arange(BLOCK)[:, None]
    place = np.arange(WINDOW)[None, :]
    angle = 2 * np.pi / WINDOW * (frequency * place % WINDOW)
    sines = -np.sin(angle)
    sines[0] = 1.0 - 2.0 * (np.arange(WINDOW) % 2)
    analysis = np.concatenate([np.cos(angle), sines], axis=0)
    taps_forward = analysis[:, :BLOCK].copy()
    taps_forward[:, taps_count:] = 0
    taps_backward = np.zeros((WINDOW, BLOCK))
    taps_backward[:, :taps_count] = taps_forward[:, :taps_count][:, ::-1]
    taps_tables = np.concatenate([taps_forward, taps_backward], axis=0)[:, :taps_count]
    out_place = np.arange(BLOCK)[:, None] + (BLOCK - taps_count)
    out_angle = 2 * np.pi / WINDOW * (out_place * np.arange(BLOCK)[None, :] % WINDOW)
    cosines = 2 * np.cos(out_angle) / WINDOW
    cosines[:, 0] = 1.0 / WINDOW
    sines = -2 * np.sin(out_angle) / WINDOW
    sines[:, 0] = (1.0 - 2.0 * (out_place[:, 0] % 2)) / WINDOW
    synthesis = np.concatenate([cosines, sines], axis=1)
    return *split_table(analysis), *split_table(taps_tables), *split_table(synthesis)


def dot(a, b):
    return jnp.dot(a, b, preferred_element_type=F32)


def gelu(v):
    return v * (0.5 + 0.5 * lax.erf(v * np.float32(np.sqrt(0.5))))


def kernel(
    acts_hbm, bases_hbm, complement_hbm, embedding_hbm, taps_hbm, weight_hbm,
    flip_hbm, fwd_hi_hbm, fwd_lo_hbm, tap_hi_hbm, tap_lo_hbm, inv_hi_hbm, inv_lo_hbm,
    out_ref,
    acts_ref, bases_ref, complement_ref, embedding_ref, taps_ref, weight_ref,
    flip_ref, fwd_hi, fwd_lo, tap_hi, tap_lo, inv_hi, inv_lo,
    halo, bases_halo, mirror, mirror_halo, weight_far,
    table, coef, rows, wide, cross, near, far,
    two_send, two_plus, two_minus, plus_send, minus_send, plus_recv, minus_recv, y_send, y_recv, y_keep,
    early_send, early_recv, early_sum, late_two, late_far,
    late_plus_send, late_minus_send, late_plus, late_minus,
    send_sem, recv_sem, local_sem,
):
    seq, tensor = lax.axis_index("seq"), lax.axis_index("tensor")
    seq_count = lax.axis_size("seq")
    z, y, core = tensor // 4, (tensor // 2) % 2, tensor % 2
    has_right, has_left = seq < seq_count - 1, seq > 0
    right, left = jnp.minimum(seq + 1, seq_count - 1), jnp.maximum(seq - 1, 0)
    opposite = 15 - tensor
    z_plus, z_minus, z_two = lax.rem(z + 1, 4), lax.rem(z + 3, 4), lax.rem(z + 2, 4)
    at_plus = (seq, z_plus * 4 + y * 2 + core)
    at_minus = (seq, z_minus * 4 + y * 2 + core)
    at_two = (seq, z_two * 4 + y * 2 + core)
    at_core = (seq, z * 4 + y * 2 + (1 - core))
    at_y = (seq, z * 4 + (1 - y) * 2 + core)
    barrier = pltpu.get_barrier_semaphore()

    def greet(*partners):
        for partner in partners:
            pl.semaphore_signal(barrier, inc=1, device_id=partner, device_id_type=MESH)

    greet((seq, opposite), at_plus, at_minus, at_core, at_y, at_two)
    pl.when(has_right)(lambda: greet((right, tensor), (right, opposite)))
    pl.when(has_left)(lambda: greet((left, tensor), (left, opposite)))
    fetched = []
    for source, target in (
        (taps_hbm, taps_ref), (tap_hi_hbm, tap_hi), (tap_lo_hbm, tap_lo), (complement_hbm, complement_ref),
        (embedding_hbm, embedding_ref), (flip_hbm, flip_ref), (weight_hbm, weight_ref), (bases_hbm, bases_ref),
        (acts_hbm, acts_ref), (fwd_hi_hbm, fwd_hi), (fwd_lo_hbm, fwd_lo), (inv_hi_hbm, inv_hi), (inv_lo_hbm, inv_lo),
    ):
        copy = pltpu.make_async_copy(source, target, local_sem.at[len(fetched)])
        copy.start()
        fetched.append(copy)

    def fetch(count):
        for copy in fetched[:count]:
            copy.wait()
        del fetched[:count]

    pl.semaphore_wait(barrier, 6 + 2 * has_right.astype(jnp.int32) + 2 * has_left.astype(jnp.int32))

    count = [0]

    def plan(source, target, device):
        index = count[0]
        count[0] += 1
        return pltpu.make_async_remote_copy(
            src_ref=source, dst_ref=target, send_sem=send_sem.at[index], recv_sem=recv_sem.at[index],
            device_id=device, device_id_type=MESH,
        )

    def send(source, target, device):
        copy = plan(source, target, device)
        copy.start()
        return copy

    length = acts_hbm.shape[0]
    first, last = pl.ds(0, LANES), pl.ds(length - LANES, LANES)
    to_right = [
        plan(acts_hbm.at[last], mirror_halo.at[0], (right, opposite)),
        plan(acts_hbm.at[last], halo.at[0], (right, tensor)),
        plan(bases_hbm, bases_halo.at[0], (right, tensor)),
    ]
    to_left = [
        plan(acts_hbm.at[first], mirror_halo.at[1], (left, opposite)),
        plan(acts_hbm.at[first], halo.at[1], (left, tensor)),
        plan(bases_hbm, bases_halo.at[1], (left, tensor)),
    ]

    def each(copies, what):
        for copy in copies:
            getattr(copy, what)()

    bounds = [0, 384, 640, 896, 1024]
    pl.when(has_right)(lambda: each(to_right, "start"))
    pieces = [
        send(acts_hbm.at[pl.ds(a, b - a)], mirror.at[pl.ds(a, b - a)], (seq, opposite))
        for a, b in zip(bounds[:-1], bounds[1:])
    ]
    pl.when(has_left)(lambda: each(to_left, "start"))
    weight_copy = send(weight_hbm, weight_far, at_core)

    def blank(side):
        halo[side] = jnp.zeros_like(halo[side])
        mirror_halo[side] = jnp.zeros_like(mirror_halo[side])
        bases_halo[side] = jnp.zeros_like(bases_halo[side])

    pl.when(jnp.logical_not(has_left))(lambda: blank(0))
    pl.when(jnp.logical_not(has_right))(lambda: blank(1))

    fetch(3)
    taps = taps_ref[...]
    spectrum = dot(tap_hi[...], taps) + dot(tap_lo[...], taps)
    for strand in range(2):
        lanes = pl.ds(strand * LANES, LANES)
        real = spectrum[strand * WINDOW : strand * WINDOW + BLOCK]
        imag = spectrum[strand * WINDOW + BLOCK : (strand + 1) * WINDOW]
        top = lax.broadcasted_iota(jnp.int32, (BLOCK, LANES), 0) == 0
        coef[0, :, lanes] = real
        coef[1, :, lanes] = jnp.where(top, 0.0, imag)
        coef[2, :, lanes] = jnp.where(top, imag, real)

    fetch(3)
    own = embedding_ref[:, pl.ds(pl.multiple_of(tensor * LANES, LANES), LANES)].astype(F32)
    vocab = own.shape[0]
    table[...] = jnp.zeros_like(table)
    for base in range(vocab):
        table[base : base + 1, 0:LANES] = own[base : base + 1]
        row = jnp.zeros((1, LANES), F32)
        for other in range(vocab):
            weight = (complement_ref[base] == other).astype(F32)
            row = row + weight * own[other : other + 1]
        table[base : base + 1, LANES:] = row
    bases_table = table[...].astype(BF16)
    flip = flip_ref[...]

    def widen(source, half):
        for z_at in range(4):
            for y_at in range(2):
                chunk = z_at * 4 + y_at * 2 + core
                columns = pl.ds(pl.multiple_of(chunk * LANES, LANES), LANES)
                mirrored = pl.ds(pl.multiple_of((15 - chunk) * LANES, LANES), LANES)
                straight, turned = source[:, columns], dot(source[:, mirrored], flip).astype(BF16)
                for part, offset in ((straight, 0), (turned, LANES)):
                    depth = pl.ds(half * BLOCK + offset, LANES)
                    wide[z_at, depth, pl.ds(y_at * LANES, LANES)] = part
                    cross[y_at, depth, pl.ds(z_at * LANES, LANES)] = part

    fetch(1)
    widen(weight_ref, 0)

    def form_rows(group):
        if group == 0:
            plain, mirrored, ids = halo[0], mirror_halo[0], bases_halo[0, 7:8, :]
            keep = has_left
        elif group == 9:
            plain, mirrored, ids = halo[1], mirror_halo[1], bases_halo[1, 0:1, :]
            keep = has_right
        else:
            part = pl.ds((group - 1) * LANES, LANES)
            plain, mirrored, ids = acts_ref[part], mirror[part], bases_ref[group - 1 : group, :]
            keep = None
        hot = (lax.broadcasted_iota(jnp.int32, (16, LANES), 0) == ids).astype(F32).astype(BF16)
        added = lax.dot_general(hot, bases_table, (((0,), (0,)), ((), ())), preferred_element_type=F32)
        both = jnp.concatenate([plain.astype(F32), dot(mirrored, flip)], axis=1) + added
        if keep is not None:
            both = jnp.where(keep, both, 0.0)
        rows[pl.ds(group * LANES, LANES), :] = both.astype(BF16)

    def conv(block):
        window = rows[pl.ds(block * BLOCK, WINDOW), :]
        field = dot(fwd_hi[...], window) + dot(fwd_lo[...], window)
        real, imag = field[:BLOCK], field[BLOCK:]
        shared = coef[1]
        product = jnp.concatenate([real * coef[0] + imag * shared, imag * coef[2] - real * shared], axis=0)
        high = product.astype(BF16)
        low = (product - high.astype(F32)).astype(BF16)
        filtered = dot(inv_hi[...], high) + dot(inv_lo[...], high) + dot(inv_hi[...], low)
        near[block] = gelu(filtered).astype(BF16)
        return send(near.at[block], far.at[block], at_core)

    def project(block, weights, low, high):
        return dot(near[block, low:high, :], weights[0:BLOCK, :]) + dot(far[block, low:high, :], weights[BLOCK:, :])

    half = BLOCK // 2
    top, bottom = pl.ds(0, half), pl.ds(half, half)
    two, plain, added, crossed = {}, {}, {}, {}

    def begin(block):
        two_send[block] = project(block, wide.at[z_two], 0, BLOCK).astype(BF16)
        two[block] = (
            send(two_send.at[block, top], two_plus.at[block], at_plus),
            send(two_send.at[block, bottom], two_minus.at[block], at_minus),
        )
        plus_send[block, half:, :] = project(block, wide.at[z_plus], half, BLOCK).astype(BF16)
        plain_plus = send(plus_send.at[block, bottom], plus_recv.at[block, bottom], at_plus)
        minus_send[block, :half, :] = project(block, wide.at[z_minus], 0, half).astype(BF16)
        plain_minus = send(minus_send.at[block, top], minus_recv.at[block, top], at_minus)
        plain[block] = (plain_plus, plain_minus)

    def accumulate(block):
        total = project(block, wide.at[z_plus], 0, half)
        two[block][0].wait_recv()
        plus_send[block, :half, :] = (total + two_plus[block].astype(F32)).astype(BF16)
        added_plus = send(plus_send.at[block, top], plus_recv.at[block, top], at_plus)
        total = project(block, wide.at[z_minus], half, BLOCK)
        two[block][1].wait_recv()
        minus_send[block, half:, :] = (total + two_minus[block].astype(F32)).astype(BF16)
        added_minus = send(minus_send.at[block, bottom], minus_recv.at[block, bottom], at_minus)
        added[block] = (added_plus, added_minus)

    def finish(block):
        total = project(block, wide.at[z], 0, BLOCK)
        for copy in plain[block] + added[block]:
            copy.wait_recv()
        total = total + plus_recv[block].astype(F32) + minus_recv[block].astype(F32)
        low, high = total[:, :LANES], total[:, LANES:]
        y_keep[block] = jnp.where(y == 0, low, high)
        y_send[block] = jnp.where(y == 0, high, low).astype(BF16)
        crossed[block] = send(y_send.at[block], y_recv.at[block], at_y)

    def emit(block):
        crossed[block].wait_recv()
        out_ref[pl.ds(block * BLOCK, BLOCK), :] = (y_keep[block] + y_recv[block].astype(F32)).astype(BF16)

    early, late = [], []

    def early_begin(block):
        for part, low in ((top, 0), (bottom, half)):
            early_send[part, :] = project(block, cross.at[1 - y], low, low + half).astype(BF16)
            early.append(send(early_send.at[part], early_recv.at[part], at_y))

    def early_middle(block):
        for index, (part, low) in enumerate(((top, 0), (bottom, half))):
            total = project(block, cross.at[y], low, low + half)
            early[index].wait_recv()
            total = total + early_recv[part, :].astype(F32)
            for z_at in range(4):
                early_sum[z_at, part, :] = total[:, z_at * LANES : (z_at + 1) * LANES]
            late_two[part, :] = early_sum[z_two, part, :].astype(BF16)
            late.append(send(late_two.at[part], late_far.at[part], at_two))
            late_plus_send[part, :] = early_sum[z_plus, part, :].astype(BF16)
            late.append(send(late_plus_send.at[part], late_plus.at[part], at_plus))
            late_minus_send[part, :] = early_sum[z_minus, part, :].astype(BF16)
            late.append(send(late_minus_send.at[part], late_minus.at[part], at_minus))

    def early_emit(block):
        each(late, "wait_recv")
        total = early_sum[z] + late_plus[...].astype(F32) + late_minus[...].astype(F32) + late_far[...].astype(F32)
        out_ref[pl.ds(block * BLOCK, BLOCK), :] = total.astype(BF16)

    fetch(6)
    cores = {}
    pl.when(has_left)(lambda: each(to_right, "wait_recv"))
    pieces[0].wait_recv()
    form_rows(0)
    form_rows(1)
    form_rows(2)
    form_rows(3)
    cores[0] = conv(0)
    pieces[1].wait_recv()
    form_rows(4)
    form_rows(5)
    cores[1] = conv(1)
    weight_copy.wait_recv()
    widen(weight_far, 1)
    cores[0].wait_recv()
    begin(0)
    cores[1].wait_recv()
    begin(1)
    pieces[2].wait_recv()
    form_rows(6)
    form_rows(7)
    cores[2] = conv(2)
    cores[2].wait_recv()
    early_begin(2)
    pl.when(has_right)(lambda: each(to_left, "wait_recv"))
    pieces[3].wait_recv()
    form_rows(8)
    form_rows(9)
    cores[3] = conv(3)
    accumulate(0)
    cores[3].wait_recv()
    begin(3)
    accumulate(1)
    accumulate(3)
    finish(0)
    early_middle(2)
    finish(1)
    finish(3)
    emit(0)
    emit(1)
    early_emit(2)
    emit(3)
    pl.when(has_right)(lambda: each(to_right, "wait_send"))
    pl.when(has_left)(lambda: each(to_left, "wait_send"))
    each(pieces + [weight_copy] + list(cores.values()) + early + late, "wait_send")
    for block in sorted(two):
        each(two[block] + plain[block] + added[block] + (crossed[block],), "wait_send")


def body(activations, bases, complement, embedding, filter_taps, projection):
    length, channels = activations.shape
    blocks = length // BLOCK
    copies = 48
    tables = dft_tables(filter_taps.shape[0])
    flip = np.eye(LANES)[::-1].astype(BF16)
    operands = [
        activations, bases.reshape(length // LANES, LANES), complement, embedding, filter_taps, projection,
        jnp.asarray(flip), *[jnp.asarray(t) for t in tables],
    ]
    vmem = pl.BlockSpec(memory_space=pltpu.VMEM)
    return pl.pallas_call(
        kernel,
        out_shape=pltpu.VMEM((length, channels), BF16),
        in_specs=[pl.BlockSpec(memory_space=pl.ANY)] * len(operands),
        out_specs=vmem,
        scratch_shapes=[
            (pltpu.SMEM if operand.ndim == 1 else pltpu.VMEM)(operand.shape, operand.dtype) for operand in operands
        ]
        + [
            pltpu.VMEM((2, LANES, LANES), BF16),
            pltpu.VMEM((2, 8, LANES), jnp.int32),
            pltpu.VMEM((length, LANES), BF16),
            pltpu.VMEM((2, LANES, LANES), BF16),
            pltpu.VMEM(projection.shape, BF16),
            pltpu.VMEM((16, 2 * LANES), F32),
            pltpu.VMEM((3, BLOCK, 2 * LANES), F32),
            pltpu.VMEM((length + 2 * LANES, 2 * LANES), BF16),
            pltpu.VMEM((4, 4 * LANES, 2 * LANES), BF16),
            pltpu.VMEM((2, 4 * LANES, 4 * LANES), BF16),
            pltpu.VMEM((blocks, BLOCK, 2 * LANES), BF16),
            pltpu.VMEM((blocks, BLOCK, 2 * LANES), BF16),
            pltpu.VMEM((blocks, BLOCK, 2 * LANES), BF16),
            pltpu.VMEM((blocks, BLOCK // 2, 2 * LANES), BF16),
            pltpu.VMEM((blocks, BLOCK // 2, 2 * LANES), BF16),
            pltpu.VMEM((blocks, BLOCK, 2 * LANES), BF16),
            pltpu.VMEM((blocks, BLOCK, 2 * LANES), BF16),
            pltpu.VMEM((blocks, BLOCK, 2 * LANES), BF16),
            pltpu.VMEM((blocks, BLOCK, 2 * LANES), BF16),
            pltpu.VMEM((blocks, BLOCK, LANES), BF16),
            pltpu.VMEM((blocks, BLOCK, LANES), BF16),
            pltpu.VMEM((blocks, BLOCK, LANES), F32),
            pltpu.VMEM((BLOCK, 4 * LANES), BF16),
            pltpu.VMEM((BLOCK, 4 * LANES), BF16),
            pltpu.VMEM((4, BLOCK, LANES), F32),
            pltpu.VMEM((BLOCK, LANES), BF16),
            pltpu.VMEM((BLOCK, LANES), BF16),
            pltpu.VMEM((BLOCK, LANES), BF16),
            pltpu.VMEM((BLOCK, LANES), BF16),
            pltpu.VMEM((BLOCK, LANES), BF16),
            pltpu.VMEM((BLOCK, LANES), BF16),
            pltpu.SemaphoreType.DMA((copies,)),
            pltpu.SemaphoreType.DMA((copies,)),
            pltpu.SemaphoreType.DMA((len(operands),)),
        ],
        compiler_params=pltpu.CompilerParams(
            collective_id=0, has_side_effects=True, vmem_limit_bytes=56 * 1024 * 1024
        ),
    )(*operands)


def solution(mesh):
    placed = (P("seq", "tensor"), P("seq"), P(), P(), P(None, "tensor"), P("tensor", None))
    return jax.shard_map(
        body, mesh=mesh, in_specs=placed, out_specs=P("seq", "tensor"), check_vma=False
    )
```

```python
import functools

import jax
import jax.numpy as jnp
import numpy as np
from jax import lax
from jax.experimental import pallas as pl
from jax.experimental.pallas import tpu as pltpu
from jax.sharding import PartitionSpec as P

MESH = pl.DeviceIdType.MESH
F32, BF16 = jnp.float32, jnp.bfloat16
LANES = 128
BLOCK = 256
WINDOW = 2 * BLOCK


def split_table(table):
    high = table.astype(BF16)
    low = (table - high.astype(np.float64)).astype(BF16)
    return high, low


def dft_tables(taps_count):
    frequency = np.arange(BLOCK)[:, None]
    place = np.arange(WINDOW)[None, :]
    angle = 2 * np.pi / WINDOW * (frequency * place % WINDOW)
    sines = -np.sin(angle)
    sines[0] = 1.0 - 2.0 * (np.arange(WINDOW) % 2)
    analysis = np.concatenate([np.cos(angle), sines], axis=0)
    taps_forward = analysis[:, :BLOCK].copy()
    taps_forward[:, taps_count:] = 0
    taps_backward = np.zeros((WINDOW, BLOCK))
    taps_backward[:, :taps_count] = taps_forward[:, :taps_count][:, ::-1]
    taps_tables = np.concatenate([taps_forward, taps_backward], axis=0)[:, :taps_count]
    out_place = np.arange(BLOCK)[:, None] + (BLOCK - taps_count)
    out_angle = 2 * np.pi / WINDOW * (out_place * np.arange(BLOCK)[None, :] % WINDOW)
    cosines = 2 * np.cos(out_angle) / WINDOW
    cosines[:, 0] = 1.0 / WINDOW
    sines = -2 * np.sin(out_angle) / WINDOW
    sines[:, 0] = (1.0 - 2.0 * (out_place[:, 0] % 2)) / WINDOW
    synthesis = np.concatenate([cosines, sines], axis=1)
    return *split_table(analysis), *split_table(taps_tables), *split_table(synthesis)


def dot(a, b):
    return jnp.dot(a, b, preferred_element_type=F32)


def gelu(v):
    return v * (0.5 + 0.5 * lax.erf(v * np.float32(np.sqrt(0.5))))


def kernel(
    acts_hbm, bases_hbm, complement_hbm, embedding_hbm, taps_hbm, weight_hbm,
    flip_hbm, fwd_hi_hbm, fwd_lo_hbm, tap_hi_hbm, tap_lo_hbm, inv_hi_hbm, inv_lo_hbm,
    out_ref,
    acts_ref, bases_ref, complement_ref, embedding_ref, taps_ref, weight_ref,
    flip_ref, fwd_hi, fwd_lo, tap_hi, tap_lo, inv_hi, inv_lo,
    halo, bases_halo, mirror, mirror_halo, weight_far,
    table, coef, rows, wide, cross, near, far,
    two_send, two_plus, two_minus, plus_send, minus_send, plus_recv, minus_recv, y_send, y_recv, y_keep,
    early_send, early_recv, early_sum, late_two, late_two_plus, late_two_minus,
    late_plus_send, late_minus_send, late_plus, late_minus,
    send_sem, recv_sem, local_sem,
):
    seq, tensor = lax.axis_index("seq"), lax.axis_index("tensor")
    seq_count = lax.axis_size("seq")
    z, y, core = tensor // 4, (tensor // 2) % 2, tensor % 2
    has_right, has_left = seq < seq_count - 1, seq > 0
    right, left = jnp.minimum(seq + 1, seq_count - 1), jnp.maximum(seq - 1, 0)
    opposite = 15 - tensor
    z_plus, z_minus, z_two = lax.rem(z + 1, 4), lax.rem(z + 3, 4), lax.rem(z + 2, 4)
    at_plus = (seq, z_plus * 4 + y * 2 + core)
    at_minus = (seq, z_minus * 4 + y * 2 + core)
    at_core = (seq, z * 4 + y * 2 + (1 - core))
    at_y = (seq, z * 4 + (1 - y) * 2 + core)
    barrier = pltpu.get_barrier_semaphore()

    def greet(*partners):
        for partner in partners:
            pl.semaphore_signal(barrier, inc=1, device_id=partner, device_id_type=MESH)

    greet((seq, opposite), at_plus, at_minus, at_core, at_y)
    pl.when(has_right)(lambda: greet((right, tensor), (right, opposite)))
    pl.when(has_left)(lambda: greet((left, tensor), (left, opposite)))
    fetched = []
    for source, target in (
        (taps_hbm, taps_ref), (tap_hi_hbm, tap_hi), (tap_lo_hbm, tap_lo), (complement_hbm, complement_ref),
        (embedding_hbm, embedding_ref), (flip_hbm, flip_ref), (weight_hbm, weight_ref), (bases_hbm, bases_ref),
        (acts_hbm, acts_ref), (fwd_hi_hbm, fwd_hi), (fwd_lo_hbm, fwd_lo), (inv_hi_hbm, inv_hi), (inv_lo_hbm, inv_lo),
    ):
        copy = pltpu.make_async_copy(source, target, local_sem.at[len(fetched)])
        copy.start()
        fetched.append(copy)

    def fetch(count):
        for copy in fetched[:count]:
            copy.wait()
        del fetched[:count]

    pl.semaphore_wait(barrier, 5 + 2 * has_right.astype(jnp.int32) + 2 * has_left.astype(jnp.int32))

    count = [0]

    def plan(source, target, device):
        index = count[0]
        count[0] += 1
        return pltpu.make_async_remote_copy(
            src_ref=source, dst_ref=target, send_sem=send_sem.at[index], recv_sem=recv_sem.at[index],
            device_id=device, device_id_type=MESH,
        )

    def send(source, target, device):
        copy = plan(source, target, device)
        copy.start()
        return copy

    length = acts_hbm.shape[0]
    first, last = pl.ds(0, LANES), pl.ds(length - LANES, LANES)
    to_right = [
        plan(acts_hbm.at[last], mirror_halo.at[0], (right, opposite)),
        plan(acts_hbm.at[last], halo.at[0], (right, tensor)),
        plan(bases_hbm, bases_halo.at[0], (right, tensor)),
    ]
    to_left = [
        plan(acts_hbm.at[first], mirror_halo.at[1], (left, opposite)),
        plan(acts_hbm.at[first], halo.at[1], (left, tensor)),
        plan(bases_hbm, bases_halo.at[1], (left, tensor)),
    ]

    def each(copies, what):
        for copy in copies:
            getattr(copy, what)()

    bounds = [0, 384, 640, 896, 1024]
    pl.when(has_right)(lambda: each(to_right, "start"))
    pieces = [
        send(acts_hbm.at[pl.ds(a, b - a)], mirror.at[pl.ds(a, b - a)], (seq, opposite))
        for a, b in zip(bounds[:-1], bounds[1:])
    ]
    pl.when(has_left)(lambda: each(to_left, "start"))
    weight_copy = send(weight_hbm, weight_far, at_core)

    def blank(side):
        halo[side] = jnp.zeros_like(halo[side])
        mirror_halo[side] = jnp.zeros_like(mirror_halo[side])
        bases_halo[side] = jnp.zeros_like(bases_halo[side])

    pl.when(jnp.logical_not(has_left))(lambda: blank(0))
    pl.when(jnp.logical_not(has_right))(lambda: blank(1))

    fetch(3)
    taps = taps_ref[...]
    spectrum = dot(tap_hi[...], taps) + dot(tap_lo[...], taps)
    for strand in range(2):
        lanes = pl.ds(strand * LANES, LANES)
        real = spectrum[strand * WINDOW : strand * WINDOW + BLOCK]
        imag = spectrum[strand * WINDOW + BLOCK : (strand + 1) * WINDOW]
        top = lax.broadcasted_iota(jnp.int32, (BLOCK, LANES), 0) == 0
        coef[0, :, lanes] = real
        coef[1, :, lanes] = jnp.where(top, 0.0, imag)
        coef[2, :, lanes] = jnp.where(top, imag, real)

    fetch(3)
    own = embedding_ref[:, pl.ds(pl.multiple_of(tensor * LANES, LANES), LANES)].astype(F32)
    vocab = own.shape[0]
    table[...] = jnp.zeros_like(table)
    for base in range(vocab):
        table[base : base + 1, 0:LANES] = own[base : base + 1]
        row = jnp.zeros((1, LANES), F32)
        for other in range(vocab):
            weight = (complement_ref[base] == other).astype(F32)
            row = row + weight * own[other : other + 1]
        table[base : base + 1, LANES:] = row
    bases_table = table[...].astype(BF16)
    flip = flip_ref[...]

    def widen(source, half):
        for z_at in range(4):
            for y_at in range(2):
                chunk = z_at * 4 + y_at * 2 + core
                columns = pl.ds(pl.multiple_of(chunk * LANES, LANES), LANES)
                mirrored = pl.ds(pl.multiple_of((15 - chunk) * LANES, LANES), LANES)
                straight, turned = source[:, columns], dot(source[:, mirrored], flip).astype(BF16)
                for part, offset in ((straight, 0), (turned, LANES)):
                    depth = pl.ds(half * BLOCK + offset, LANES)
                    wide[z_at, depth, pl.ds(y_at * LANES, LANES)] = part
                    cross[y_at, depth, pl.ds(z_at * LANES, LANES)] = part

    fetch(1)
    widen(weight_ref, 0)

    def form_rows(group):
        if group == 0:
            plain, mirrored, ids = halo[0], mirror_halo[0], bases_halo[0, 7:8, :]
            keep = has_left
        elif group == 9:
            plain, mirrored, ids = halo[1], mirror_halo[1], bases_halo[1, 0:1, :]
            keep = has_right
        else:
            part = pl.ds((group - 1) * LANES, LANES)
            plain, mirrored, ids = acts_ref[part], mirror[part], bases_ref[group - 1 : group, :]
            keep = None
        hot = (lax.broadcasted_iota(jnp.int32, (16, LANES), 0) == ids).astype(F32).astype(BF16)
        added = lax.dot_general(hot, bases_table, (((0,), (0,)), ((), ())), preferred_element_type=F32)
        both = jnp.concatenate([plain.astype(F32), dot(mirrored, flip)], axis=1) + added
        if keep is not None:
            both = jnp.where(keep, both, 0.0)
        rows[pl.ds(group * LANES, LANES), :] = both.astype(BF16)

    def conv(block):
        window = rows[pl.ds(block * BLOCK, WINDOW), :]
        field = dot(fwd_hi[...], window) + dot(fwd_lo[...], window)
        real, imag = field[:BLOCK], field[BLOCK:]
        shared = coef[1]
        product = jnp.concatenate([real * coef[0] + imag * shared, imag * coef[2] - real * shared], axis=0)
        high = product.astype(BF16)
        low = (product - high.astype(F32)).astype(BF16)
        filtered = dot(inv_hi[...], high) + dot(inv_lo[...], high) + dot(inv_hi[...], low)
        near[block] = gelu(filtered).astype(BF16)
        return send(near.at[block], far.at[block], at_core)

    def project(block, weights, low, high):
        return dot(near[block, low:high, :], weights[0:BLOCK, :]) + dot(far[block, low:high, :], weights[BLOCK:, :])

    half = BLOCK // 2
    top, bottom = pl.ds(0, half), pl.ds(half, half)
    two, plain, added, crossed = {}, {}, {}, {}

    def begin(block):
        two_send[block, :half, :] = project(block, wide.at[z_two], 0, half).astype(BF16)
        upper = send(two_send.at[block, top], two_plus.at[block], at_plus)
        two_send[block, half:, :] = project(block, wide.at[z_two], half, BLOCK).astype(BF16)
        two[block] = (upper, send(two_send.at[block, bottom], two_minus.at[block], at_minus))
        plus_send[block, half:, :] = project(block, wide.at[z_plus], half, BLOCK).astype(BF16)
        plain_plus = send(plus_send.at[block, bottom], plus_recv.at[block, bottom], at_plus)
        minus_send[block, :half, :] = project(block, wide.at[z_minus], 0, half).astype(BF16)
        plain_minus = send(minus_send.at[block, top], minus_recv.at[block, top], at_minus)
        plain[block] = (plain_plus, plain_minus)

    def accumulate(block):
        total = project(block, wide.at[z_plus], 0, half)
        two[block][0].wait_recv()
        plus_send[block, :half, :] = (total + two_plus[block].astype(F32)).astype(BF16)
        added_plus = send(plus_send.at[block, top], plus_recv.at[block, top], at_plus)
        total = project(block, wide.at[z_minus], half, BLOCK)
        two[block][1].wait_recv()
        minus_send[block, half:, :] = (total + two_minus[block].astype(F32)).astype(BF16)
        added_minus = send(minus_send.at[block, bottom], minus_recv.at[block, bottom], at_minus)
        added[block] = (added_plus, added_minus)

    def finish(block):
        total = project(block, wide.at[z], 0, BLOCK)
        for copy in plain[block] + added[block]:
            copy.wait_recv()
        total = total + plus_recv[block].astype(F32) + minus_recv[block].astype(F32)
        low, high = total[:, :LANES], total[:, LANES:]
        y_keep[block] = jnp.where(y == 0, low, high)
        y_send[block] = jnp.where(y == 0, high, low).astype(BF16)
        crossed[block] = send(y_send.at[block], y_recv.at[block], at_y)

    def emit(block):
        crossed[block].wait_recv()
        out_ref[pl.ds(block * BLOCK, BLOCK), :] = (y_keep[block] + y_recv[block].astype(F32)).astype(BF16)

    early, late = [], []

    def early_begin(block):
        for part, low in ((top, 0), (bottom, half)):
            early_send[part, :] = project(block, cross.at[1 - y], low, low + half).astype(BF16)
            early.append(send(early_send.at[part], early_recv.at[part], at_y))

    def early_middle(block):
        for index, (part, low) in enumerate(((top, 0), (bottom, half))):
            total = project(block, cross.at[y], low, low + half)
            early[index].wait_recv()
            total = total + early_recv[part, :].astype(F32)
            for z_at in range(4):
                early_sum[z_at, part, :] = total[:, z_at * LANES : (z_at + 1) * LANES]
            late_two[part, :] = early_sum[z_two, part, :].astype(BF16)
            if index == 0:
                late.append(send(late_two.at[top], late_two_plus, at_plus))
                late_minus_send[top, :] = early_sum[z_minus, top, :].astype(BF16)
                late.append(send(late_minus_send.at[top], late_minus.at[top], at_minus))
            else:
                late.append(send(late_two.at[bottom], late_two_minus, at_minus))
                late_plus_send[bottom, :] = early_sum[z_plus, bottom, :].astype(BF16)
                late.append(send(late_plus_send.at[bottom], late_plus.at[bottom], at_plus))

    def early_accumulate():
        late[0].wait_recv()
        late_plus_send[top, :] = (early_sum[z_plus, top, :] + late_two_plus[...].astype(F32)).astype(BF16)
        late.append(send(late_plus_send.at[top], late_plus.at[top], at_plus))
        late[2].wait_recv()
        late_minus_send[bottom, :] = (early_sum[z_minus, bottom, :] + late_two_minus[...].astype(F32)).astype(BF16)
        late.append(send(late_minus_send.at[bottom], late_minus.at[bottom], at_minus))

    def early_emit(block):
        for index in (1, 3, 4, 5):
            late[index].wait_recv()
        total = early_sum[z] + late_plus[...].astype(F32) + late_minus[...].astype(F32)
        out_ref[pl.ds(block * BLOCK, BLOCK), :] = total.astype(BF16)

    fetch(6)
    cores = {}
    pl.when(has_left)(lambda: each(to_right, "wait_recv"))
    pieces[0].wait_recv()
    form_rows(0)
    form_rows(1)
    form_rows(2)
    form_rows(3)
    cores[0] = conv(0)
    pieces[1].wait_recv()
    form_rows(4)
    form_rows(5)
    cores[1] = conv(1)
    weight_copy.wait_recv()
    widen(weight_far, 1)
    cores[0].wait_recv()
    begin(0)
    cores[1].wait_recv()
    begin(1)
    pieces[2].wait_recv()
    form_rows(6)
    form_rows(7)
    cores[2] = conv(2)
    cores[2].wait_recv()
    early_begin(2)
    pl.when(has_right)(lambda: each(to_left, "wait_recv"))
    pieces[3].wait_recv()
    form_rows(8)
    form_rows(9)
    cores[3] = conv(3)
    accumulate(0)
    cores[3].wait_recv()
    begin(3)
    accumulate(1)
    accumulate(3)
    early_middle(2)
    finish(0)
    finish(1)
    early_accumulate()
    finish(3)
    emit(0)
    emit(1)
    early_emit(2)
    emit(3)
    pl.when(has_right)(lambda: each(to_right, "wait_send"))
    pl.when(has_left)(lambda: each(to_left, "wait_send"))
    each(pieces + [weight_copy] + list(cores.values()) + early + late, "wait_send")
    for block in sorted(two):
        each(two[block] + plain[block] + added[block] + (crossed[block],), "wait_send")


def body(activations, bases, complement, embedding, filter_taps, projection):
    length, channels = activations.shape
    blocks = length // BLOCK
    copies = 48
    tables = dft_tables(filter_taps.shape[0])
    flip = np.eye(LANES)[::-1].astype(BF16)
    operands = [
        activations, bases.reshape(length // LANES, LANES), complement, embedding, filter_taps, projection,
        jnp.asarray(flip), *[jnp.asarray(t) for t in tables],
    ]
    vmem = pl.BlockSpec(memory_space=pltpu.VMEM)
    return pl.pallas_call(
        kernel,
        out_shape=pltpu.VMEM((length, channels), BF16),
        in_specs=[pl.BlockSpec(memory_space=pl.ANY)] * len(operands),
        out_specs=vmem,
        scratch_shapes=[
            (pltpu.SMEM if operand.ndim == 1 else pltpu.VMEM)(operand.shape, operand.dtype) for operand in operands
        ]
        + [
            pltpu.VMEM((2, LANES, LANES), BF16),
            pltpu.VMEM((2, 8, LANES), jnp.int32),
            pltpu.VMEM((length, LANES), BF16),
            pltpu.VMEM((2, LANES, LANES), BF16),
            pltpu.VMEM(projection.shape, BF16),
            pltpu.VMEM((16, 2 * LANES), F32),
            pltpu.VMEM((3, BLOCK, 2 * LANES), F32),
            pltpu.VMEM((length + 2 * LANES, 2 * LANES), BF16),
            pltpu.VMEM((4, 4 * LANES, 2 * LANES), BF16),
            pltpu.VMEM((2, 4 * LANES, 4 * LANES), BF16),
            pltpu.VMEM((blocks, BLOCK, 2 * LANES), BF16),
            pltpu.VMEM((blocks, BLOCK, 2 * LANES), BF16),
            pltpu.VMEM((blocks, BLOCK, 2 * LANES), BF16),
            pltpu.VMEM((blocks, BLOCK // 2, 2 * LANES), BF16),
            pltpu.VMEM((blocks, BLOCK // 2, 2 * LANES), BF16),
            pltpu.VMEM((blocks, BLOCK, 2 * LANES), BF16),
            pltpu.VMEM((blocks, BLOCK, 2 * LANES), BF16),
            pltpu.VMEM((blocks, BLOCK, 2 * LANES), BF16),
            pltpu.VMEM((blocks, BLOCK, 2 * LANES), BF16),
            pltpu.VMEM((blocks, BLOCK, LANES), BF16),
            pltpu.VMEM((blocks, BLOCK, LANES), BF16),
            pltpu.VMEM((blocks, BLOCK, LANES), F32),
            pltpu.VMEM((BLOCK, 4 * LANES), BF16),
            pltpu.VMEM((BLOCK, 4 * LANES), BF16),
            pltpu.VMEM((4, BLOCK, LANES), F32),
            pltpu.VMEM((BLOCK, LANES), BF16),
            pltpu.VMEM((BLOCK // 2, LANES), BF16),
            pltpu.VMEM((BLOCK // 2, LANES), BF16),
            pltpu.VMEM((BLOCK, LANES), BF16),
            pltpu.VMEM((BLOCK, LANES), BF16),
            pltpu.VMEM((BLOCK, LANES), BF16),
            pltpu.VMEM((BLOCK, LANES), BF16),
            pltpu.SemaphoreType.DMA((copies,)),
            pltpu.SemaphoreType.DMA((copies,)),
            pltpu.SemaphoreType.DMA((len(operands),)),
        ],
        compiler_params=pltpu.CompilerParams(
            collective_id=0, has_side_effects=True, vmem_limit_bytes=56 * 1024 * 1024
        ),
    )(*operands)


def solution(mesh):
    placed = (P("seq", "tensor"), P("seq"), P(), P(), P(None, "tensor"), P("tensor", None))
    return jax.shard_map(
        body, mesh=mesh, in_specs=placed, out_specs=P("seq", "tensor"), check_vma=False
    )
```
